128 devices in a mesh: ma: 32 (over y, x, core), oct: 4 (over z).
Axes of the slice: x: 4, y: 4, z: 4, core: 2. Of those that a mesh axis runs over, the one named last changes fastest.
Arguments:
- fourier_wind: bfloat16 [2560, 64, 512], P(('ma', 'oct')), may hold values from -6 to 6
- quad_weight: float32 [2560], P('oct'), may hold values from 0.3 to 3
- p_table: bfloat16 [64, 2560, 2560], P('ma', 'oct'), may hold values from -0.125 to 0.125
- h_table: bfloat16 [64, 2560, 2560], P('ma', 'oct'), may hold values from -0.125 to 0.125
- wavenumbers: int32 [64], P('ma'), may hold values from 639 to 1921, as said below
- row_latitude: int32 [2560], replicated, may hold values from 0 to 2559, as said below
Outputs:
- rotational: bfloat16 [2560, 64, 512], P(('ma', 'oct'))
- divergent: bfloat16 [2560, 64, 512], P(('ma', 'oct'))
The draws below stay inside these ranges and needn't reach their ends.
Inputs may be any that keep to these rules, and one draw needn't show every extreme that they name: Slots come in pairs 2 d and 2 d + 1 holding wavenumbers w and 2560 - w, with w between 639 and 1278; all wavenumbers distinct. `row_latitude`: A permutation; the rows of index o along oct (rows i with (i // 20) % (2560 // 640) == o) hold exactly the latitudes o * 640 to (o + 1) * 640 - 1.
All inputs are finite; a program needn't handle non-finite values.
Results may differ from the reference program's by a relative error of at most 0.0056.
Values may be sent and summed in bfloat16 or wider, within the bound.
No kernel may reach another device: no remote copies, remote signals or barrier semaphores. Data moves between devices by JAX's collectives and lax.ppermute only.
A program may use at most 128 MiB of HBM per device.

```python
import math
import jax
import jax.numpy as jnp
from jax import lax

LMAX = 2559
NLAT = 2560
K = 128
NL = 2560
M = 64
QLAT = 640
ROWS = 20


def draw_wavenumbers(key, part):
    key = jax.random.fold_in(key, 3)
    span = LMAX // 4
    picked = jax.random.permutation(key, span)[:M // 2]
    picked = picked - jnp.min(picked) + LMAX // 4
    return jnp.stack([picked, LMAX + 1 - picked], axis=1).reshape(-1).astype(jnp.int32)


def draw_row_latitude(key, part):
    key = jax.random.fold_in(key, 5)
    groups = NLAT // QLAT
    owners = QLAT // ROWS
    keys = jax.random.split(key, groups)
    perms = jax.vmap(lambda one: jax.random.permutation(one, QLAT))(keys)
    perms = perms + jnp.arange(groups)[:, None] * QLAT
    return jnp.transpose(perms.reshape(groups, owners, ROWS), (1, 0, 2)).reshape(-1).astype(jnp.int32)


def block_scale(stream_key, extent, cuts, low, high):
    def one(axis_at, blocks):
        steps = jax.random.uniform(jax.random.fold_in(jax.random.fold_in(stream_key, 6), axis_at), (blocks,), jnp.float32, low / len(cuts), high / len(cuts))
        return jnp.repeat(jnp.exp(steps), extent[axis_at] // blocks).reshape((-1,) + (1,) * (len(extent) - axis_at - 1))

    gain = one(*cuts[0])
    for cut in cuts[1:]:
        gain = gain * one(*cut)
    return gain


def bell_draw(own_key, shape, scale, most, pieces=(), kind=jnp.bfloat16):
    entries = scale * jax.random.normal(own_key, shape, jnp.float32)
    if pieces:
        entries = entries * block_scale(own_key, shape, pieces, -0.22, 0.18)
    return jnp.clip(entries, -most, most).astype(kind)


def setup_inputs(seed: int = 0) -> dict:
    seeds = jax.random.split(jax.random.key(seed), 7)
    fourier_wind = bell_draw(seeds[0], (NLAT, M, 4 * K), 1.0, 6.0, ((0, 128),))
    quad_weight = jnp.clip(jnp.exp(math.log(3.0) - 2.3025851 * jax.random.uniform(seeds[1], (NLAT,), jnp.float32) ** block_scale(seeds[1], (NLAT,), ((0, 4),), -0.2, 0.2)), 0.3, 3.0)
    p_table = bell_draw(seeds[2], (M, NLAT, NL), NLAT ** -0.5, 0.125, ((0, 32), (1, 4)))
    h_table = bell_draw(seeds[3], (M, NLAT, NL), NLAT ** -0.5, 0.125, ((0, 32), (1, 4)))
    wavenumbers = draw_wavenumbers(jax.random.fold_in(seeds[6], 71), 0)
    row_latitude = draw_row_latitude(jax.random.fold_in(seeds[6], 71), 0)
    return {"fourier_wind": fourier_wind, "quad_weight": quad_weight, "p_table": p_table, "h_table": h_table, "wavenumbers": wavenumbers, "row_latitude": row_latitude}


def reference(fourier_wind, quad_weight, p_table, h_table, wavenumbers, row_latitude):
    by_lat = jnp.zeros_like(fourier_wind).at[row_latitude].set(fourier_wind)
    weighted = (quad_weight[:, None, None] * by_lat.astype(jnp.float32)).astype(jnp.bfloat16)
    weighted = jnp.transpose(weighted, (1, 0, 2))
    levels = fourier_wind.shape[2] // 4
    degree = jnp.arange(LMAX + 1).astype(jnp.float32)

    def one_slot(items):
        p_slot, h_slot, w_slot, number = items
        rate = number.astype(jnp.float32) / LMAX
        proj_p = jnp.dot(p_slot.T, w_slot, preferred_element_type=jnp.float32).reshape(-1, 4, levels)
        proj_h = jnp.dot(h_slot.T, w_slot, preferred_element_type=jnp.float32).reshape(-1, 4, levels)
        spectra = jnp.stack([
            -rate * proj_p[:, 3] + proj_h[:, 0],
            rate * proj_p[:, 2] + proj_h[:, 1],
            -rate * proj_p[:, 1] - proj_h[:, 2],
            rate * proj_p[:, 0] - proj_h[:, 3]], axis=1)
        factor = jnp.where(degree >= number.astype(jnp.float32),
                           -(LMAX * LMAX * 1.0) / jnp.maximum(degree * (degree + 1.0), 1.0), 0.0)
        potentials = (spectra * factor[:, None, None]).reshape(-1, 4 * levels).astype(jnp.bfloat16)
        back_p = jnp.dot(p_slot, potentials, preferred_element_type=jnp.float32).reshape(-1, 4, levels)
        back_h = jnp.dot(h_slot, potentials, preferred_element_type=jnp.float32).reshape(-1, 4, levels)
        rot = jnp.stack([-back_h[:, 0], -back_h[:, 1], -rate * back_p[:, 1], rate * back_p[:, 0]], axis=1)
        div = jnp.stack([-rate * back_p[:, 3], rate * back_p[:, 2], back_h[:, 2], back_h[:, 3]], axis=1)
        return rot.reshape(-1, 4 * levels).astype(jnp.bfloat16), div.reshape(-1, 4 * levels).astype(jnp.bfloat16)

    rot_all, div_all = lax.map(one_slot, (p_table, h_table, weighted, wavenumbers))
    rotational = jnp.transpose(rot_all, (1, 0, 2))[row_latitude]
    divergent = jnp.transpose(div_all, (1, 0, 2))[row_latitude]
    return rotational, divergent
```

```python
import functools

import jax
import jax.numpy as jnp
from jax import lax
from jax.experimental import pallas as pl
from jax.experimental.pallas import tpu as pltpu
from jax.sharding import PartitionSpec as P

LMAX = 2559
TILE = 128
GROUP = 3
PACK = 4
BF16 = jnp.bfloat16
F32 = jnp.float32
VMEM = 40 * 1024 * 1024


def dot(a, b, dims):
    return lax.dot_general(a, b, (dims, ((), ())), preferred_element_type=F32)


def pack_kernel(first_ref, second_ref, out_ref, wide_ref):
    rows, slots, lanes = first_ref.shape
    size = PACK * slots
    i = lax.broadcasted_iota(jnp.int32, (size, size), 0)
    j = lax.broadcasted_iota(jnp.int32, (size, size), 1)
    source = ((i >> 1) & (PACK - 1)) * slots + (i >> 3) * 2 + (i & 1)
    order = jnp.where(source == j, 1.0, 0.0).astype(BF16)
    for b in range(rows // PACK):
        for at, ref in enumerate((first_ref, second_ref)):
            block = ref[b * PACK:(b + 1) * PACK].reshape(size, lanes)
            moved = dot(order, block, ((1,), (0,)))
            wide_ref[:, 8 * b:8 * b + 8, at * lanes:(at + 1) * lanes] = moved.reshape(slots // 2, 8, lanes)
    out_ref[...] = wide_ref[...].astype(BF16)


def pack(wind, first, second):
    rows, slots, width = wind.shape
    lanes = width // 4
    return pl.pallas_call(
        pack_kernel,
        grid=(1,),
        out_shape=jax.ShapeDtypeStruct((slots // 2, rows * 2, 2 * lanes), BF16),
        in_specs=[
            pl.BlockSpec((rows, slots, lanes), lambda i: (0, 0, first)),
            pl.BlockSpec((rows, slots, lanes), lambda i: (0, 0, second)),
        ],
        out_specs=pl.BlockSpec((slots // 2, rows * 2, 2 * lanes), lambda i: (0, 0, 0)),
        scratch_shapes=[pltpu.VMEM((slots // 2, rows * 2, 2 * lanes), F32)],
        compiler_params=pltpu.CompilerParams(vmem_limit_bytes=VMEM),
        name="pack",
    )(wind, wind)


def unpack_kernel(rot_in, div_in, *refs):
    rot_out, div_out, wide_ref = refs[-3:]
    rows, slots, lanes = rot_out.shape
    size = PACK * slots
    i = lax.broadcasted_iota(jnp.int32, (size, size), 0)
    j = lax.broadcasted_iota(jnp.int32, (size, size), 1)
    slot = i & (slots - 1)
    source = (slot >> 1) * 8 + (i // slots) * 2 + (slot & 1)
    order = jnp.where(source == j, 1.0, 0.0).astype(BF16)
    for ref, out in ((rot_in, rot_out), (div_in, div_out)):
        wide_ref[...] = ref[...].astype(F32)
        for b in range(rows // PACK):
            block = wide_ref[:, 8 * b:8 * b + 8, :].reshape(size, lanes).astype(BF16)
            moved = dot(order, block, ((1,), (0,)))
            out[b * PACK:(b + 1) * PACK] = moved.reshape(PACK, slots, lanes).astype(BF16)


def unpack(payload, rows, base, stride, previous=()):
    pairs, both, width = payload.shape
    lanes = width // 4
    slots = pairs * 2
    shape = jax.ShapeDtypeStruct((rows, slots, width), BF16)
    out_spec = pl.BlockSpec((rows, slots, lanes), lambda i: (0, 0, base + stride * i))
    return pl.pallas_call(
        unpack_kernel,
        grid=(2,),
        out_shape=(shape, shape),
        in_specs=[
            pl.BlockSpec((pairs, both, lanes), lambda i: (0, 0, i)),
            pl.BlockSpec((pairs, both, lanes), lambda i: (0, 0, 2 + i)),
        ] + [pl.BlockSpec(memory_space=pl.ANY)] * len(previous),
        out_specs=(out_spec, out_spec),
        scratch_shapes=[pltpu.VMEM((pairs, both, lanes), F32)],
        input_output_aliases={2: 0, 3: 1} if previous else {},
        compiler_params=pltpu.CompilerParams(vmem_limit_bytes=VMEM),
        name="unpack",
    )(payload, payload, *previous)


def forward_kernel(meta, rate, recv, select, weight, *refs):
    p_refs, h_refs = refs[:GROUP], refs[GROUP:2 * GROUP]
    own, x1a, x1b, x2a, x2b, x3a, x3b, wind, spec = refs[2 * GROUP:]
    step = pl.program_id(0)
    quarter = wind.shape[2]
    levels = spec.shape[0] // 2

    @pl.when(step == 0)
    def _():
        by_lat = dot(recv[...], select[...], ((0,), (0,)))
        weighted = (by_lat * weight[...]).astype(BF16)
        wind[0] = weighted[:, :quarter]
        wind[1] = weighted[:, quarter:]

    base = step * GROUP
    first = meta[base]
    last = meta[base + GROUP - 1]

    def tile(slot, p, h):
        w = wind[slot]
        r = rate[slot]
        proj_p = dot(w, p, ((1,), (0,)))
        proj_h = dot(w, h, ((1,), (0,)))
        return (proj_h[:levels] - r * proj_p[levels:], r * proj_p[:levels] - proj_h[levels:])

    @pl.when(first == last)
    def _():
        psi, chi = tile(
            first,
            jnp.concatenate([ref[0] for ref in p_refs], axis=1),
            jnp.concatenate([ref[0] for ref in h_refs], axis=1),
        )
        spec[:levels] = psi
        spec[levels:] = chi

    @pl.when(first != last)
    def _():
        for k in range(GROUP):
            psi, chi = tile(meta[base + k], p_refs[k][0], h_refs[k][0])
            spec[:levels, k * TILE:(k + 1) * TILE] = psi
            spec[levels:, k * TILE:(k + 1) * TILE] = chi

    me = meta[meta.shape[0] - 1]
    chunk = own.shape[0]
    half = chunk // 2

    def part(k, at, size):
        start = lax.rem(me + k, 4) * chunk + at
        return spec[pl.ds(pl.multiple_of(start, half), size), :]

    own[...] = part(0, 0, chunk)
    x1a[...] = part(1, 0, half)
    x1b[...] = part(1, half, half).astype(BF16)
    x2a[...] = part(2, 0, half).astype(BF16)
    x2b[...] = part(2, half, half).astype(BF16)
    x3a[...] = part(3, 0, half).astype(BF16)
    x3b[...] = part(3, half, half)


def table_specs(quarter, n_tiles):
    def at(k):
        return lambda i, meta: (meta[i * GROUP + k], 0, meta[n_tiles + i * GROUP + k])

    return [pl.BlockSpec((1, quarter, TILE), at(k)) for k in range(GROUP)]


def forward(meta, rate, recv, select, weight, p_table, h_table, n_tiles):
    quarter = p_table.shape[1]
    both, width = recv.shape
    degrees = n_tiles * TILE
    chunk = width // 4
    half = chunk // 2
    shapes = [(chunk, F32), (half, F32), (half, BF16), (half, BF16), (half, BF16), (half, BF16), (half, F32)]
    once = pl.Buffered(1)
    return pl.pallas_call(
        forward_kernel,
        grid_spec=pltpu.PrefetchScalarGridSpec(
            num_scalar_prefetch=1,
            grid=(n_tiles // GROUP,),
            in_specs=[
                pl.BlockSpec(memory_space=pltpu.SMEM),
                pl.BlockSpec((both, width), lambda i, meta: (0, 0), pipeline_mode=once),
                pl.BlockSpec((both, both), lambda i, meta: (0, 0), pipeline_mode=once),
                pl.BlockSpec((1, both), lambda i, meta: (0, 0), pipeline_mode=once),
            ] + table_specs(quarter, n_tiles) * 2,
            out_specs=[pl.BlockSpec((n, GROUP * TILE), lambda i, meta: (0, i)) for n, _ in shapes],
            scratch_shapes=[
                pltpu.VMEM((2, width, quarter), BF16),
                pltpu.VMEM((width, GROUP * TILE), F32),
            ],
        ),
        out_shape=[jax.ShapeDtypeStruct((n, degrees), t) for n, t in shapes],
        compiler_params=pltpu.CompilerParams(vmem_limit_bytes=VMEM),
        cost_estimate=pl.CostEstimate(flops=6 * 10**9, bytes_accessed=16 * 10**6, transcendentals=0),
        name="forward",
    )(meta, rate, recv, select, weight, *([p_table] * GROUP), *([h_table] * GROUP))


def backward_kernel(meta, rate, select, *refs):
    parts, refs = refs[:8], refs[8:]
    p_refs, h_refs = refs[:GROUP], refs[GROUP:2 * GROUP]
    out, potential, sum_p, sum_h, winds = refs[2 * GROUP:]
    step = pl.program_id(0)
    quarter = sum_p.shape[1]
    levels = potential.shape[0] // 2
    me = meta[meta.shape[0] - 1]
    half = parts[0].shape[0]

    @pl.when(step == 0)
    def _():
        sum_p[...] = jnp.zeros_like(sum_p)
        sum_h[...] = jnp.zeros_like(sum_h)

    for n, ref in enumerate(parts):
        start = (lax.rem(me + n // 2, 4) * 2 + n % 2) * half
        potential[pl.ds(pl.multiple_of(start, half), half), :] = ref[...]

    base = step * GROUP
    first = meta[base]
    last = meta[base + GROUP - 1]

    @pl.when(first == last)
    def _():
        pot = potential[...]
        sum_p[first] += dot(jnp.concatenate([ref[0] for ref in p_refs], axis=1), pot, ((1,), (1,)))
        sum_h[first] += dot(jnp.concatenate([ref[0] for ref in h_refs], axis=1), pot, ((1,), (1,)))

    @pl.when(first != last)
    def _():
        for k in range(GROUP):
            pot = potential[:, k * TILE:(k + 1) * TILE]
            sum_p[meta[base + k]] += dot(p_refs[k][0], pot, ((1,), (1,)))
            sum_h[meta[base + k]] += dot(h_refs[k][0], pot, ((1,), (1,)))

    @pl.when(step == pl.num_programs(0) - 1)
    def _():
        for slot in range(2):
            r = rate[slot]
            rows = slice(slot * quarter, (slot + 1) * quarter)
            winds[rows, 0 * levels:1 * levels] = (-sum_h[slot, :, :levels]).astype(BF16)
            winds[rows, 1 * levels:2 * levels] = (r * sum_p[slot, :, :levels]).astype(BF16)
            winds[rows, 2 * levels:3 * levels] = (-r * sum_p[slot, :, levels:]).astype(BF16)
            winds[rows, 3 * levels:4 * levels] = sum_h[slot, :, levels:].astype(BF16)
        out[...] = dot(select[...], winds[...], ((1,), (0,))).astype(BF16)


def backward(meta, rate, select, parts, p_table, h_table, n_tiles):
    quarter = p_table.shape[1]
    half = parts[0].shape[0]
    width = half * 8
    both = select.shape[0]
    return pl.pallas_call(
        backward_kernel,
        grid_spec=pltpu.PrefetchScalarGridSpec(
            num_scalar_prefetch=1,
            grid=(n_tiles // GROUP,),
            in_specs=[
                pl.BlockSpec(memory_space=pltpu.SMEM),
                pl.BlockSpec((both, both), lambda i, meta: (0, 0), pipeline_mode=pl.Buffered(1)),
            ] + [pl.BlockSpec((half, GROUP * TILE), lambda i, meta: (0, i))] * 8
            + table_specs(quarter, n_tiles) * 2,
            out_specs=pl.BlockSpec((both, 2 * width), lambda i, meta: (0, 0)),
            scratch_shapes=[
                pltpu.VMEM((width, GROUP * TILE), BF16),
                pltpu.VMEM((2, quarter, width), F32),
                pltpu.VMEM((2, quarter, width), F32),
                pltpu.VMEM((both, 2 * width), BF16),
            ],
        ),
        out_shape=jax.ShapeDtypeStruct((both, 2 * width), BF16),
        compiler_params=pltpu.CompilerParams(vmem_limit_bytes=VMEM),
        cost_estimate=pl.CostEstimate(flops=6 * 10**9, bytes_accessed=16 * 10**6, transcendentals=0),
        name="backward",
    )(meta, rate, select, *parts, *([p_table] * GROUP), *([h_table] * GROUP))


def on_device(fourier_wind, quad_weight, p_table, h_table, wavenumbers, row_latitude):
    owners = lax.axis_size("ma")
    groups = lax.axis_size("oct")
    me = lax.axis_index("oct")
    rows = fourier_wind.shape[0]
    quarter = p_table.shape[1]
    degrees = p_table.shape[2]
    count = degrees // TILE
    n_tiles = count + 1
    up = [(i, (i + 1) % groups) for i in range(groups)]
    down = [(i, (i - 1) % groups) for i in range(groups)]

    sent = [pack(fourier_wind, 0, 3), pack(fourier_wind, 1, 2)]
    received = [lax.all_to_all(x, "ma", 0, 0, tiled=True) for x in sent]

    low = wavenumbers[0] // TILE
    n_first = count - low
    start = wavenumbers[1] // TILE
    t = jnp.arange(n_tiles)
    slot = (t >= n_first).astype(jnp.int32)
    tile_at = jnp.where(slot == 0, low + t, start + t - n_first)
    real = tile_at < count
    tile_at = jnp.minimum(tile_at, count - 1)
    meta = jnp.concatenate([slot, tile_at, me[None]]).astype(jnp.int32)
    rate = wavenumbers.astype(F32) / LMAX

    degree = (tile_at[:, None] * TILE + jnp.arange(TILE)[None, :]).astype(F32)
    limit = jnp.where(slot == 0, wavenumbers[0], wavenumbers[1]).astype(F32)[:, None]
    factor = jnp.where(
        (degree >= limit) & real[:, None],
        -(LMAX * LMAX * 1.0) / jnp.maximum(degree * (degree + 1.0), 1.0),
        0.0,
    ).reshape(1, n_tiles * TILE)

    local = lax.dynamic_index_in_dim(row_latitude.reshape(owners, groups, rows), me, 1, keepdims=False) - me * quarter
    target = (local[:, :, None] + quarter * jnp.arange(2)[None, None, :]).reshape(-1, 1)
    select = (target == jnp.arange(2 * quarter)[None, :]).astype(BF16)
    weight = jnp.concatenate([quad_weight, quad_weight]).reshape(1, -1)

    outs = []
    for n in range(2):
        sign = rate if n == 0 else -rate
        own, x1a, x1b, x2a, x2b, x3a, x3b = forward(
            meta, sign, received[n].reshape(2 * quarter, -1), select, weight, p_table, h_table, n_tiles)
        half = x1a.shape[0]
        a = lax.ppermute(x2a, "oct", up)
        b = lax.ppermute(x2b, "oct", down)
        c = lax.ppermute(x1b, "oct", up)
        d = lax.ppermute(x3a, "oct", down)
        a = lax.ppermute((a.astype(F32) + x1a).astype(BF16), "oct", up)
        b = lax.ppermute((b.astype(F32) + x3b).astype(BF16), "oct", down)
        pot_a = ((own[:half] + a.astype(F32) + d.astype(F32)) * factor).astype(BF16)
        pot_b = ((own[half:] + c.astype(F32) + b.astype(F32)) * factor).astype(BF16)
        below_a = lax.ppermute(pot_a, "oct", up)
        above_b = lax.ppermute(pot_b, "oct", down)
        below_b = lax.ppermute(pot_b, "oct", up)
        above_a = lax.ppermute(pot_a, "oct", down)
        far_a = lax.ppermute(below_a, "oct", up)
        far_b = lax.ppermute(above_b, "oct", down)
        parts = (pot_a, pot_b, above_a, above_b, far_a, far_b, below_a, below_b)
        payload = backward(meta, sign, select, parts, p_table, h_table, n_tiles)
        outs.append(lax.all_to_all(payload.reshape(owners, 2 * rows, -1), "ma", 0, 0, tiled=True))

    done = unpack(outs[0], rows, 0, 3)
    return tuple(unpack(outs[1], rows, 1, 1, done))


def solution(mesh):
    placed = (
        P(("ma", "oct"), None, None),
        P("oct"),
        P("ma", "oct", None),
        P("ma", "oct", None),
        P("ma"),
        P(),
    )
    return jax.shard_map(
        on_device,
        mesh=mesh,
        in_specs=placed,
        out_specs=(P(("ma", "oct"), None, None), P(("ma", "oct"), None, None)),
        check_vma=False,
    )
```

```python
import functools

import jax
import jax.numpy as jnp
from jax import lax
from jax.experimental import pallas as pl
from jax.experimental.pallas import tpu as pltpu
from jax.sharding import PartitionSpec as P

LMAX = 2559
TILE = 128
SURE = (11, 5)
SHARED = 5
KEPT = SURE[0] + SHARED + SURE[1]
BLOCK = 512
BF16 = jnp.bfloat16
F32 = jnp.float32
LIMIT = 32 * 1024 * 1024
IN_VMEM = pl.BlockSpec(memory_space=pltpu.VMEM)
IN_SMEM = pl.BlockSpec(memory_space=pltpu.SMEM)
IN_PLACE = pl.BlockSpec(memory_space=pl.ANY)
NN = ((1,), (0,))
TN = ((0,), (0,))
NT = ((1,), (1,))


def dot(a, b, dims):
    return lax.dot_general(a, b, (dims, ((), ())), preferred_element_type=F32)


def call(kernel, name, **kwargs):
    return pl.pallas_call(
        kernel, name=name, compiler_params=pltpu.CompilerParams(vmem_limit_bytes=LIMIT), **kwargs)


def one_hot(index):
    size = index.shape[0]
    return jnp.where(index == lax.broadcasted_iota(jnp.int32, (size, size), 1), 1.0, 0.0).astype(BF16)


def pack_kernel(wind_ref, out_ref, wide_ref, order8, order4):
    rows, slots, lanes = wind_ref.shape

    @pl.when(pl.program_id(0) == 0)
    def _():
        for count, order in ((8, order8), (4, order4)):
            i = lax.broadcasted_iota(jnp.int32, order.shape, 0)
            order[...] = one_hot((i % count) * slots + (i // (2 * count)) * 2 + (i // count) % 2)

    for start in (0, 8, 16):
        count, order = (8, order8) if start < 16 else (4, order4)
        block = wind_ref[start:start + count].reshape(count * slots, lanes)
        moved = dot(order[...], block, NN).reshape(slots // 2, 2 * count, lanes)
        if start < 16:
            wide_ref[:, start:start + 8] = moved[:, :8]
            wide_ref[:, 16 + start:24 + start] = moved[:, 8:]
        else:
            wide_ref[:, 32:] = moved
    out_ref[...] = wide_ref[...].astype(BF16)


def pack(wind):
    rows, slots, width = wind.shape
    lanes = width // 2
    block = (slots // 2, rows * 2, lanes)
    return call(
        pack_kernel,
        "pack",
        grid=(2,),
        out_shape=pltpu.HBM((slots // 2, rows * 2, width), BF16),
        in_specs=[pl.BlockSpec((rows, slots, lanes), lambda i: (0, 0, i))],
        out_specs=pl.BlockSpec(block, lambda i: (0, 0, i)),
        scratch_shapes=[
            pltpu.VMEM(block, F32),
            pltpu.VMEM((8 * slots, 8 * slots), BF16),
            pltpu.VMEM((4 * slots, 4 * slots), BF16),
        ],
    )(*in_hbm(wind))


def unpack_kernel(rot_in, div_in, rot_out, div_out, wide_ref, order8, order4):
    rows, slots, lanes = rot_out.shape

    @pl.when(pl.program_id(0) == 0)
    def _():
        for count, order in ((8, order8), (4, order4)):
            i = lax.broadcasted_iota(jnp.int32, order.shape, 0)
            slot = i % slots
            order[...] = one_hot((slot // 2) * (2 * count) + (slot % 2) * count + i // slots)

    for ref, out in ((rot_in, rot_out), (div_in, div_out)):
        wide_ref[...] = ref[...].astype(F32)
        for start in (0, 8, 16):
            if start < 16:
                block = jnp.concatenate([wide_ref[:, start:start + 8], wide_ref[:, 16 + start:24 + start]], axis=1)
                count, order = 8, order8
            else:
                block = wide_ref[:, 32:]
                count, order = 4, order4
            moved = dot(order[...], block.reshape(count * slots, lanes).astype(BF16), NN)
            out[start:start + count] = moved.reshape(count, slots, lanes).astype(BF16)


def unpack(payload, rows):
    pairs, both, width = payload.shape
    lanes = width // 8
    slots = pairs * 2
    shape = jax.ShapeDtypeStruct((rows, slots, width // 2), BF16)

    def column(i):
        return jnp.where(i == 0, 0, jnp.where(i == 3, 1, i + 3))

    out_spec = pl.BlockSpec((rows, slots, lanes), lambda i: (0, 0, i))
    return call(
        unpack_kernel,
        "unpack",
        grid=(4,),
        out_shape=(shape, shape),
        in_specs=[
            pl.BlockSpec((pairs, both, lanes), lambda i: (0, 0, column(i))),
            pl.BlockSpec((pairs, both, lanes), lambda i: (0, 0, column(i) + 2)),
        ],
        out_specs=(out_spec, out_spec),
        scratch_shapes=[
            pltpu.VMEM((pairs, both, lanes), F32),
            pltpu.VMEM((8 * slots, 8 * slots), BF16),
            pltpu.VMEM((4 * slots, 4 * slots), BF16),
        ],
    )(payload, payload)


def in_hbm(*arrays):
    return [pltpu.with_memory_space_constraint(x, pltpu.HBM) for x in arrays]


def keep_kernel(meta, p_ref, h_ref, out_ref, sems):
    quarter, degrees = p_ref.shape[1:]
    pieces = [(0, degrees - SURE[0] * TILE, SURE[0], 0)]
    for k in range(SHARED):
        pieces.append((meta[k], pl.multiple_of(meta[SHARED + k] * TILE, TILE), 1, SURE[0] + k))
    pieces.append((1, degrees - SURE[1] * TILE, SURE[1], SURE[0] + SHARED))
    copies = []
    for slot, source, count, target in pieces:
        for at, ref in enumerate((p_ref, h_ref)):
            copies.append(pltpu.make_async_copy(
                ref.at[slot, :, pl.ds(source, count * TILE)],
                out_ref.at[pl.ds(at * quarter, quarter), pl.ds(target * TILE, count * TILE)],
                sems.at[len(copies)],
            ))
            copies[-1].start()
    for copy in copies:
        copy.wait()


def keep(meta, p_table, h_table):
    shape = (2 * p_table.shape[1], KEPT * TILE)
    return call(
        keep_kernel,
        "keep",
        out_shape=pltpu.VMEM(shape, BF16),
        in_specs=[IN_SMEM] + [IN_PLACE] * 2,
        out_specs=IN_VMEM,
        scratch_shapes=[pltpu.SemaphoreType.DMA((2 * (2 + SHARED),))],
    )(meta, *in_hbm(p_table, h_table))


def forward_kernel(part, meta, rate, mask, weight, recv, select, table, keep, send, wide, wind, spec):
    owners, both, width = wide.shape
    quarter = select.shape[2]
    levels = width // 2
    main = owners * 16
    for n, at in enumerate((part, 3 - part)):
        wide[:, :, n * levels:(n + 1) * levels] = recv[:, :, at * levels:(at + 1) * levels].astype(F32)
    mixed = wide[:, 32:].reshape(owners * 8, width).astype(BF16)
    for slot in range(2):
        rows = wide[:, 16 * slot:16 * slot + 16].reshape(main, width).astype(BF16)
        by_lat = dot(rows, select[slot, :main], TN) + dot(mixed, select[slot, main:], TN)
        wind[slot] = (by_lat * weight[...]).astype(BF16)
    split = (SURE[0] + SHARED) * TILE
    for slot in range(2):
        low, high = (0, split) if slot == 0 else (SURE[0] * TILE, KEPT * TILE)
        r = rate[slot]
        w = wind[slot]
        for start in range(low, high, BLOCK):
            cols = slice(start, min(start + BLOCK, high))
            proj_p = dot(w, table[:quarter, cols], NN)
            proj_h = dot(w, table[quarter:, cols], NN)
            psi = proj_h[:levels] - r * proj_p[levels:]
            chi = r * proj_p[:levels] - proj_h[levels:]
            if slot == 1 and start < split:
                first = mask[:, cols] > 0.5
                psi = jnp.where(first, spec[:levels, cols], psi)
                chi = jnp.where(first, spec[levels:, cols], chi)
            spec[:levels, cols] = psi
            spec[levels:, cols] = chi
    mine = meta[2 * SHARED] * levels
    keep[...] = spec[pl.ds(pl.multiple_of(mine, levels), levels), :]
    send[...] = spec[pl.ds(pl.multiple_of(levels - mine, levels), levels), :].astype(BF16)


def forward(part, meta, rate, mask, weight, recv, select, table):
    owners, both, width = recv.shape
    levels = width // 4
    quarter = select.shape[2]
    degrees = table.shape[1]
    return call(
        functools.partial(forward_kernel, part),
        "forward",
        in_specs=[IN_SMEM] * 2 + [IN_VMEM] * 5,
        out_specs=[IN_VMEM] * 2,
        out_shape=[jax.ShapeDtypeStruct((levels, degrees), F32), jax.ShapeDtypeStruct((levels, degrees), BF16)],
        scratch_shapes=[
            pltpu.VMEM((owners, both, 2 * levels), F32),
            pltpu.VMEM((2, 2 * levels, quarter), BF16),
            pltpu.VMEM((2 * levels, degrees), F32),
        ],
    )(meta, rate, mask, weight, recv, select, table)


def backward_kernel(part, meta, rate, mask, mine, theirs, select, table, *refs):
    out_ref, every, masked, winds, wide, out, sem = refs[-7:]
    levels = mine.shape[0]
    quarter = select.shape[2]
    owners, both, width = out.shape
    main = owners * 16
    split = (SURE[0] + SHARED) * TILE
    degrees = KEPT * TILE
    at = meta[2 * SHARED] * levels
    every[pl.ds(pl.multiple_of(at, levels), levels), :] = mine[...]
    every[pl.ds(pl.multiple_of(levels - at, levels), levels), :] = theirs[...]
    shared = slice(SURE[0] * TILE, split)
    first = mask[:, shared] > 0.5
    both_slots = every[:, shared].astype(F32)
    masked[0, :, :shared.start] = every[:, :shared.start]
    masked[0, :, shared] = jnp.where(first, both_slots, 0.0).astype(BF16)
    masked[1, :, :split - shared.start] = jnp.where(first, 0.0, both_slots).astype(BF16)
    masked[1, :, split - shared.start:degrees - shared.start] = every[:, split:]
    for slot in range(2):
        low, high = (0, split) if slot == 0 else (shared.start, degrees)
        pot = masked[slot, :, :high - low]
        sums = [dot(table[n * quarter:(n + 1) * quarter, low:high], pot, NT) for n in range(2)]
        r = rate[slot]
        winds[slot, :, :levels] = (-sums[1][:, :levels]).astype(BF16)
        winds[slot, :, levels:2 * levels] = (r * sums[0][:, :levels]).astype(BF16)
        winds[slot, :, 2 * levels:3 * levels] = (-r * sums[0][:, levels:]).astype(BF16)
        winds[slot, :, 3 * levels:] = sums[1][:, levels:].astype(BF16)
    for slot in range(2):
        moved = dot(select[slot, :main], winds[slot], NN)
        wide[:, 16 * slot:16 * slot + 16] = moved.reshape(owners, 16, width)
    mixed = dot(select[0, main:], winds[0], NN) + dot(select[1, main:], winds[1], NN)
    wide[:, 32:] = mixed.reshape(owners, 8, width)
    out[...] = wide[...].astype(BF16)
    copy = pltpu.make_async_copy(out, out_ref.at[:, :, pl.ds(part * width, width)], sem)
    copy.start()
    copy.wait()


def backward(part, meta, rate, mask, mine, theirs, select, table, payload, filled=()):
    quarter = select.shape[2]
    levels, degrees = mine.shape
    owners, both, width = payload
    piece = (owners, both, width // 2)
    return call(
        functools.partial(backward_kernel, part),
        "backward",
        in_specs=[IN_SMEM] * 2 + [IN_VMEM] * 5 + [IN_PLACE] * len(filled),
        out_specs=IN_PLACE,
        out_shape=pltpu.HBM(payload, BF16),
        input_output_aliases={7: 0} if filled else {},
        scratch_shapes=[
            pltpu.VMEM((2 * levels, degrees), BF16),
            pltpu.VMEM((2, 2 * levels, (SURE[0] + SHARED) * TILE), BF16),
            pltpu.VMEM((2, quarter, width // 2), BF16),
            pltpu.VMEM(piece, F32),
            pltpu.VMEM(piece, BF16),
            pltpu.SemaphoreType.DMA,
        ],
    )(meta, rate, mask, mine, theirs, select, table, *filled)


def add_kernel(kept, got, total, sent):
    total[...] = kept[...] + got[...].astype(F32)
    sent[...] = total[...].astype(BF16)


def add(kept, got):
    return call(
        add_kernel,
        "add",
        in_specs=[IN_VMEM] * 2,
        out_specs=[IN_VMEM] * 2,
        out_shape=[jax.ShapeDtypeStruct(kept.shape, F32), jax.ShapeDtypeStruct(kept.shape, BF16)],
    )(kept, got)


def scale_kernel(kept, got, factor, mine):
    mine[...] = ((kept[...] + got[...].astype(F32)) * factor[...]).astype(BF16)


def scale(kept, got, factor):
    return call(
        scale_kernel,
        "scale",
        in_specs=[IN_VMEM] * 3,
        out_specs=IN_VMEM,
        out_shape=jax.ShapeDtypeStruct(kept.shape, BF16),
    )(kept, got, factor)


def on_device(fourier_wind, quad_weight, p_table, h_table, wavenumbers, row_latitude):
    owners = lax.axis_size("ma")
    groups = lax.axis_size("oct")
    me = lax.axis_index("oct")
    rows = fourier_wind.shape[0]
    quarter = p_table.shape[1]
    count = p_table.shape[2] // TILE
    flip, turn = [z ^ 1 for z in range(groups)], [groups - 1 - z for z in range(groups)]
    first = [
        (d * groups + z, d * groups + (flip, turn)[d % 2][z]) for d in range(owners) for z in range(groups)]
    second = [
        (d * groups + z, d * groups + (turn, flip)[d % 2][z]) for d in range(owners) for z in range(groups)]
    half = jnp.where(lax.axis_index("ma") % 2 == 0, ((me + 1) // 2) % 2, me // 2)

    def swap(x, pairs):
        return lax.ppermute(x, ("ma", "oct"), pairs)

    received = lax.all_to_all(pack(fourier_wind), "ma", 0, 0, tiled=True)

    n_first = count - wavenumbers[0] // TILE - SURE[0]
    k = jnp.arange(SHARED)
    shared_slot = (k >= n_first).astype(jnp.int32)
    shared_tile = jnp.where(k < n_first, count - SURE[0] - 1 - k, count - SURE[1] - 1 - (k - n_first))
    meta = jnp.concatenate([shared_slot, shared_tile, half[None]]).astype(jnp.int32)
    slot = jnp.concatenate([jnp.zeros(SURE[0], jnp.int32), shared_slot, jnp.ones(SURE[1], jnp.int32)])
    tile = jnp.concatenate([jnp.arange(count - SURE[0], count), shared_tile, jnp.arange(count - SURE[1], count)])
    mask = jnp.repeat(1.0 - slot.astype(F32), TILE)[None, :]
    degree = (tile[:, None] * TILE + jnp.arange(TILE)[None, :]).astype(F32)
    limit = jnp.where(slot == 0, wavenumbers[0], wavenumbers[1]).astype(F32)[:, None]
    factor = jnp.where(
        degree >= limit, -(LMAX * LMAX * 1.0) / jnp.maximum(degree * (degree + 1.0), 1.0), 0.0).reshape(1, -1)
    rate = wavenumbers.astype(F32) / LMAX

    local = lax.dynamic_index_in_dim(row_latitude.reshape(owners, groups, rows), me, 1, keepdims=False) - me * quarter
    none = jnp.full((owners, 4), -1, jnp.int32)
    main, last = local[:, :16].reshape(-1), local[:, 16:]
    target = jnp.stack([
        jnp.concatenate([main, jnp.concatenate([last, none], axis=1).reshape(-1)]),
        jnp.concatenate([main, jnp.concatenate([none, last], axis=1).reshape(-1)]),
    ])
    select = (target[:, :, None] == jnp.arange(quarter)[None, None, :]).astype(BF16)
    weight = quad_weight.reshape(1, -1)

    table = pltpu.with_memory_space_constraint(keep(meta, p_table, h_table), pltpu.VMEM)
    owners, both, width = received.shape
    payload = (owners, both, 2 * width)
    signs = (rate, -rate)
    mines, theirs = [], []
    for n in range(2):
        kept, sent = forward(n, meta, signs[n], mask, weight, received, select, table)
        kept, sent = add(kept, swap(sent, first))
        mines.append(scale(kept, swap(sent, second), factor))
        theirs.append(swap(mines[n], first))
    filled = ()
    for n in range(2):
        filled = (backward(n, meta, signs[n], mask, mines[n], theirs[n], select, table, payload, filled),)
    return tuple(unpack(lax.all_to_all(filled[0], "ma", 0, 0, tiled=True), rows))


def solution(mesh):
    placed = (
        P(("ma", "oct"), None, None),
        P("oct"),
        P("ma", "oct", None),
        P("ma", "oct", None),
        P("ma"),
        P(),
    )
    return jax.shard_map(
        on_device,
        mesh=mesh,
        in_specs=placed,
        out_specs=(P(("ma", "oct"), None, None), P(("ma", "oct"), None, None)),
        check_vma=False,
    )
```

```python
import functools

import jax
import jax.numpy as jnp
from jax import lax
from jax.experimental import pallas as pl
from jax.experimental.pallas import tpu as pltpu
from jax.sharding import PartitionSpec as P

LMAX = 2559
TILE = 128
SURE = (11, 5)
SHARED = 5
KEPT = SURE[0] + SHARED + SURE[1]
BLOCK = 512
BF16 = jnp.bfloat16
F32 = jnp.float32
LIMIT = 32 * 1024 * 1024
IN_VMEM = pl.BlockSpec(memory_space=pltpu.VMEM)
IN_SMEM = pl.BlockSpec(memory_space=pltpu.SMEM)
IN_PLACE = pl.BlockSpec(memory_space=pl.ANY)
NN = ((1,), (0,))
TN = ((0,), (0,))
NT = ((1,), (1,))


def dot(a, b, dims):
    return lax.dot_general(a, b, (dims, ((), ())), preferred_element_type=F32)


def call(kernel, name, **kwargs):
    return pl.pallas_call(
        kernel, name=name, compiler_params=pltpu.CompilerParams(vmem_limit_bytes=LIMIT), **kwargs)


def fill_order(order, source):
    size = order.shape[0]
    index = source(lax.broadcasted_iota(jnp.int32, (size, 1), 0))
    hit = index == lax.broadcasted_iota(jnp.int32, (size, size), 1)
    order[...] = jnp.where(hit, 1.0, 0.0).astype(BF16)


def log2(n):
    return n.bit_length() - 1


def pack_kernel(wind_ref, out_ref, order8, order4):
    rows, slots, lanes = wind_ref.shape

    @pl.when(pl.program_id(0) == 0)
    def _():
        for count, order in ((8, order8), (4, order4)):
            c = log2(count)
            fill_order(order, lambda i: (i & (count - 1)) * slots + ((i >> (c + 1)) << 1) + ((i >> c) & 1))

    eights = []
    for start in (0, 8, 16):
        count, order = (8, order8) if start < 16 else (4, order4)
        block = wind_ref[start:start + count].reshape(count * slots, lanes)
        eights.append(dot(order[...], block, NN).reshape(slots // 2, 2 * count, lanes))
    for slot in range(2):
        rows_of = [x[:, 8 * slot:8 * slot + 8] for x in eights[:2]]
        out_ref[:, 16 * slot:16 * slot + 16] = jnp.concatenate(rows_of, axis=1).astype(BF16)
    out_ref[:, 32:] = eights[2].astype(BF16)


def pack(wind):
    rows, slots, width = wind.shape
    lanes = width // 2
    return call(
        pack_kernel,
        "pack",
        grid=(2,),
        out_shape=pltpu.HBM((slots // 2, rows * 2, width), BF16),
        in_specs=[pl.BlockSpec((rows, slots, lanes), lambda i: (0, 0, i))],
        out_specs=pl.BlockSpec((slots // 2, rows * 2, lanes), lambda i: (0, 0, i)),
        scratch_shapes=[
            pltpu.VMEM((8 * slots, 8 * slots), BF16),
            pltpu.VMEM((4 * slots, 4 * slots), BF16),
        ],
    )(*in_hbm(wind))


def unpack_kernel(payload, rot_ref, div_ref, outs, order8, order4, sems):
    _, rows, slots, width = outs.shape
    lanes = width // 4
    for count, order in ((8, order8), (4, order4)):
        c = log2(count)

        def source(i):
            slot = i & (slots - 1)
            return ((slot >> 1) << (c + 1)) + ((slot & 1) << c) + (i >> log2(slots))

        fill_order(order, source)
    copies = []
    for n, component in enumerate((0, 3, 1, 2)):
        cols = slice(2 * n * lanes, 2 * (n + 1) * lanes)
        mains = [payload[:, 16 * slot:16 * slot + 16, cols].astype(F32) for slot in range(2)]
        for start in (0, 8, 16):
            if start < 16:
                block = jnp.concatenate([x[:, start:start + 8] for x in mains], axis=1)
                count, order = 8, order8
            else:
                block = payload[:, 32:, cols].astype(F32)
                count, order = 4, order4
            moved = dot(order[...], block.reshape(count * slots, 2 * lanes).astype(BF16), NN)
            moved = moved.reshape(count, slots, 2 * lanes).astype(BF16)
            for k, ref in enumerate((rot_ref, div_ref)):
                outs[k, start:start + count, :, component * lanes:(component + 1) * lanes] = (
                    moved[:, :, k * lanes:(k + 1) * lanes])
                at = (pl.ds(start, count), slice(None), pl.ds(component * lanes, lanes))
                copies.append(pltpu.make_async_copy(outs.at[(k, *at)], ref.at[at], sems.at[len(copies)]))
                copies[-1].start()
    for copy in copies:
        copy.wait()


def unpack(payload, rows):
    pairs, both, width = payload.shape
    slots = pairs * 2
    shape = (rows, slots, width // 2)
    return call(
        unpack_kernel,
        "unpack",
        out_shape=(pltpu.HBM(shape, BF16), pltpu.HBM(shape, BF16)),
        in_specs=[IN_VMEM],
        out_specs=(IN_PLACE, IN_PLACE),
        scratch_shapes=[
            pltpu.VMEM((2, *shape), BF16),
            pltpu.VMEM((8 * slots, 8 * slots), BF16),
            pltpu.VMEM((4 * slots, 4 * slots), BF16),
            pltpu.SemaphoreType.DMA((24,)),
        ],
    )(payload)


def in_hbm(*arrays):
    return [pltpu.with_memory_space_constraint(x, pltpu.HBM) for x in arrays]


def keep_kernel(meta, p_ref, h_ref, out_ref, kept, sems, out_sems):
    quarter, degrees = p_ref.shape[1:]
    pieces = [(0, degrees - SURE[0] * TILE, SURE[0], 0)]
    for k in range(SHARED):
        pieces.append((meta[k], pl.multiple_of(meta[SHARED + k] * TILE, TILE), 1, SURE[0] + k))
    pieces.append((1, degrees - SURE[1] * TILE, SURE[1], SURE[0] + SHARED))
    copies = []
    for at, ref in enumerate((p_ref, h_ref)):
        for slot, source, count, target in pieces:
            copies.append(pltpu.make_async_copy(
                ref.at[slot, :, pl.ds(source, count * TILE)],
                kept.at[pl.ds(at * quarter, quarter), pl.ds(target * TILE, count * TILE)],
                sems.at[len(copies)],
            ))
            copies[-1].start()
    sent = []
    for at in range(2):
        for copy in copies[at * len(pieces):(at + 1) * len(pieces)]:
            copy.wait()
        rows = pl.ds(at * quarter, quarter)
        sent.append(pltpu.make_async_copy(kept.at[rows], out_ref.at[rows], out_sems.at[at]))
        sent[at].start()
    for copy in sent:
        copy.wait()


def keep(meta, p_table, h_table):
    shape = (2 * p_table.shape[1], KEPT * TILE)
    return call(
        keep_kernel,
        "keep",
        out_shape=pltpu.HBM(shape, BF16),
        in_specs=[IN_SMEM] + [IN_PLACE] * 2,
        out_specs=IN_PLACE,
        scratch_shapes=[
            pltpu.VMEM(shape, BF16),
            pltpu.SemaphoreType.DMA((2 * (2 + SHARED),)),
            pltpu.SemaphoreType.DMA((2,)),
        ],
    )(meta, *in_hbm(p_table, h_table))


STREAM = 512
N_BLOCKS = -(-KEPT * TILE // STREAM)


def forward_kernel(part, meta, rate, mask, weight, recv, select, table, keep, send, *refs):
    owners, both, width = recv.shape
    source, (table, wind, spec, sems) = table, refs
    copies = []
    for n in range(N_BLOCKS):
        cols = pl.ds(n * STREAM, min(STREAM, KEPT * TILE - n * STREAM))
        copies.append(pltpu.make_async_copy(source.at[:, cols], table.at[:, cols], sems.at[n]))
        copies[n].start()
    waited = 0
    quarter = select.shape[2]
    levels = width // 4
    main = owners * 16
    columns = [slice(at * levels, (at + 1) * levels) for at in (part, 3 - part)]
    mixed = [recv[:, 32:, cols].astype(F32).reshape(owners * 8, levels).astype(BF16) for cols in columns]
    for slot in range(2):
        rows = [recv[:, 16 * slot:16 * slot + 16, cols].reshape(main, levels) for cols in columns]
        by_lat = dot(jnp.concatenate(rows, axis=1), select[slot, :main], TN)
        by_lat = by_lat + dot(jnp.concatenate(mixed, axis=1), select[slot, main:], TN)
        wind[slot] = (by_lat * weight[...]).astype(BF16)
    split = (SURE[0] + SHARED) * TILE
    for slot in range(2):
        low, high = (0, split) if slot == 0 else (SURE[0] * TILE, KEPT * TILE)
        r = rate[slot]
        w = wind[slot]
        for start in range(low, high, BLOCK):
            cols = slice(start, min(start + BLOCK, high))
            while waited < len(copies) and waited * STREAM < cols.stop:
                copies[waited].wait()
                waited += 1
            proj_p = dot(w, table[:quarter, cols], NN)
            proj_h = dot(w, table[quarter:, cols], NN)
            psi = proj_h[:levels] - r * proj_p[levels:]
            chi = r * proj_p[:levels] - proj_h[levels:]
            if slot == 1 and start < split:
                first = mask[:, cols] > 0.5
                psi = jnp.where(first, spec[:levels, cols], psi)
                chi = jnp.where(first, spec[levels:, cols], chi)
            spec[:levels, cols] = psi
            spec[levels:, cols] = chi
    mine = meta[2 * SHARED] * levels
    keep[...] = spec[pl.ds(pl.multiple_of(mine, levels), levels), :]
    send[...] = spec[pl.ds(pl.multiple_of(levels - mine, levels), levels), :].astype(BF16)


def forward(part, meta, rate, mask, weight, recv, select, table):
    owners, both, width = recv.shape
    levels = width // 4
    quarter = select.shape[2]
    degrees = table.shape[1]
    out_shape = [jax.ShapeDtypeStruct((levels, degrees), F32), jax.ShapeDtypeStruct((levels, degrees), BF16)]
    scratch = [
        pltpu.VMEM((2, 2 * levels, quarter), BF16),
        pltpu.VMEM((2 * levels, degrees), F32),
        pltpu.SemaphoreType.DMA((N_BLOCKS,)),
    ]
    (scratch, out_shape)[part].insert((0, 2)[part], pltpu.VMEM(table.shape, BF16))
    return call(
        functools.partial(forward_kernel, part),
        "forward",
        in_specs=[IN_SMEM] * 2 + [IN_VMEM] * 4 + [IN_PLACE],
        out_specs=[IN_VMEM] * len(out_shape),
        out_shape=out_shape,
        scratch_shapes=scratch,
        cost_estimate=pl.CostEstimate(flops=5 * 10**9, bytes_accessed=10**7, transcendentals=0),
    )(meta, rate, mask, weight, recv, select, *in_hbm(table))


def backward_kernel(part, meta, rate, mask, mine, theirs, select, table, *refs):
    out_ref, every, masked, winds, out, sems = refs[-6:]
    levels = mine.shape[0]
    quarter = select.shape[2]
    owners, both, width = out.shape
    main = owners * 16
    split = (SURE[0] + SHARED) * TILE
    degrees = KEPT * TILE
    at = meta[2 * SHARED] * levels
    every[pl.ds(pl.multiple_of(at, levels), levels), :] = mine[...]
    every[pl.ds(pl.multiple_of(levels - at, levels), levels), :] = theirs[...]
    shared = slice(SURE[0] * TILE, split)
    first = mask[:, shared] > 0.5
    both_slots = every[:, shared].astype(F32)
    masked[0, :, :shared.start] = every[:, :shared.start]
    masked[0, :, shared] = jnp.where(first, both_slots, 0.0).astype(BF16)
    masked[1, :, :split - shared.start] = jnp.where(first, 0.0, both_slots).astype(BF16)
    masked[1, :, split - shared.start:degrees - shared.start] = every[:, split:]
    for slot in range(2):
        low, high = (0, split) if slot == 0 else (shared.start, degrees)
        pot = masked[slot, :, :high - low]
        sums = [dot(table[n * quarter:(n + 1) * quarter, low:high], pot, NT) for n in range(2)]
        r = rate[slot]
        winds[slot, :, :levels] = (-sums[1][:, :levels]).astype(BF16)
        winds[slot, :, levels:2 * levels] = (-r * sums[0][:, levels:]).astype(BF16)
        winds[slot, :, 2 * levels:3 * levels] = (r * sums[0][:, :levels]).astype(BF16)
        winds[slot, :, 3 * levels:] = sums[1][:, levels:].astype(BF16)
    copies = []
    for n in range(2):
        cols = slice(n * width // 2, (n + 1) * width // 2)
        for slot in range(2):
            moved = dot(select[slot, :main], winds[slot, :, cols], NN)
            out[:, 16 * slot:16 * slot + 16, cols] = moved.astype(BF16).reshape(owners, 16, width // 2)
        mixed = dot(select[0, main:], winds[0, :, cols], NN) + dot(select[1, main:], winds[1, :, cols], NN)
        out[:, 32:, cols] = mixed.reshape(owners, 8, width // 2).astype(BF16)
        copies.append(pltpu.make_async_copy(
            out.at[:, :, pl.ds(n * width // 2, width // 2)],
            out_ref.at[:, :, pl.ds(part * width + n * width // 2, width // 2)],
            sems.at[n],
        ))
        copies[n].start()
    for copy in copies:
        copy.wait()


def backward(part, meta, rate, mask, mine, theirs, select, table, payload, filled=()):
    quarter = select.shape[2]
    levels, degrees = mine.shape
    owners, both, width = payload
    piece = (owners, both, width // 2)
    return call(
        functools.partial(backward_kernel, part),
        "backward",
        in_specs=[IN_SMEM] * 2 + [IN_VMEM] * 5 + [IN_PLACE] * len(filled),
        out_specs=IN_PLACE,
        out_shape=pltpu.HBM(payload, BF16),
        input_output_aliases={7: 0} if filled else {},
        scratch_shapes=[
            pltpu.VMEM((2 * levels, degrees), BF16),
            pltpu.VMEM((2, 2 * levels, (SURE[0] + SHARED) * TILE), BF16),
            pltpu.VMEM((2, quarter, width // 2), BF16),
            pltpu.VMEM(piece, BF16),
            pltpu.SemaphoreType.DMA((2,)),
        ],
    )(meta, rate, mask, mine, theirs, select, table, *filled)


def add_kernel(kept, got, total, sent):
    total[...] = kept[...] + got[...].astype(F32)
    sent[...] = total[...].astype(BF16)


def add(kept, got):
    return call(
        add_kernel,
        "add",
        in_specs=[IN_VMEM] * 2,
        out_specs=[IN_VMEM] * 2,
        out_shape=[jax.ShapeDtypeStruct(kept.shape, F32), jax.ShapeDtypeStruct(kept.shape, BF16)],
    )(kept, got)


def scale_kernel(kept, got, factor, mine):
    mine[...] = ((kept[...] + got[...].astype(F32)) * factor[...]).astype(BF16)


def scale(kept, got, factor):
    return call(
        scale_kernel,
        "scale",
        in_specs=[IN_VMEM] * 3,
        out_specs=IN_VMEM,
        out_shape=jax.ShapeDtypeStruct(kept.shape, BF16),
    )(kept, got, factor)


def on_device(fourier_wind, quad_weight, p_table, h_table, wavenumbers, row_latitude):
    owners = lax.axis_size("ma")
    groups = lax.axis_size("oct")
    me = lax.axis_index("oct")
    rows = fourier_wind.shape[0]
    quarter = p_table.shape[1]
    count = p_table.shape[2] // TILE
    flip, turn = [z ^ 1 for z in range(groups)], [groups - 1 - z for z in range(groups)]
    first = [
        (d * groups + z, d * groups + (flip, turn)[d % 2][z]) for d in range(owners) for z in range(groups)]
    second = [
        (d * groups + z, d * groups + (turn, flip)[d % 2][z]) for d in range(owners) for z in range(groups)]
    half = jnp.where(lax.axis_index("ma") % 2 == 0, ((me + 1) // 2) % 2, me // 2)

    def swap(x, pairs):
        return lax.ppermute(x, ("ma", "oct"), pairs)

    received = lax.all_to_all(pack(fourier_wind), "ma", 0, 0, tiled=True)

    n_first = count - wavenumbers[0] // TILE - SURE[0]
    k = jnp.arange(SHARED)
    shared_slot = (k >= n_first).astype(jnp.int32)
    shared_tile = jnp.where(k < n_first, count - SURE[0] - 1 - k, count - SURE[1] - 1 - (k - n_first))
    meta = jnp.concatenate([shared_slot, shared_tile, half[None]]).astype(jnp.int32)
    slot = jnp.concatenate([jnp.zeros(SURE[0], jnp.int32), shared_slot, jnp.ones(SURE[1], jnp.int32)])
    tile = jnp.concatenate([jnp.arange(count - SURE[0], count), shared_tile, jnp.arange(count - SURE[1], count)])
    mask = jnp.repeat(1.0 - slot.astype(F32), TILE)[None, :]
    degree = (tile[:, None] * TILE + jnp.arange(TILE)[None, :]).astype(F32)
    limit = jnp.where(slot == 0, wavenumbers[0], wavenumbers[1]).astype(F32)[:, None]
    factor = jnp.where(
        degree >= limit, -(LMAX * LMAX * 1.0) / jnp.maximum(degree * (degree + 1.0), 1.0), 0.0).reshape(1, -1)
    rate = wavenumbers.astype(F32) / LMAX

    local = lax.dynamic_index_in_dim(row_latitude.reshape(owners, groups, rows), me, 1, keepdims=False) - me * quarter
    none = jnp.full((owners, 4), -1, jnp.int32)
    main, last = local[:, :16].reshape(-1), local[:, 16:]
    target = jnp.stack([
        jnp.concatenate([main, jnp.concatenate([last, none], axis=1).reshape(-1)]),
        jnp.concatenate([main, jnp.concatenate([none, last], axis=1).reshape(-1)]),
    ])
    select = (target[:, :, None] == jnp.arange(quarter)[None, None, :]).astype(BF16)
    weight = quad_weight.reshape(1, -1)

    table = keep(meta, p_table, h_table)
    owners, both, width = received.shape
    payload = (owners, both, 2 * width)
    signs = (rate, -rate)
    kept_a, sent_a = forward(0, meta, signs[0], mask, weight, received, select, table)
    kept_b, sent_b, table = forward(1, meta, signs[1], mask, weight, received, select, table)
    table = pltpu.with_memory_space_constraint(table, pltpu.VMEM)
    kept_a, sent_a = add(kept_a, swap(sent_a, first))
    kept_b, sent_b = add(kept_b, swap(sent_b, first))
    mine_a = scale(kept_a, swap(sent_a, second), factor)
    mine_b = scale(kept_b, swap(sent_b, second), factor)
    out = backward(0, meta, signs[0], mask, mine_a, swap(mine_a, first), select, table, payload)
    out = backward(1, meta, signs[1], mask, mine_b, swap(mine_b, first), select, table, payload, (out,))
    return tuple(unpack(lax.all_to_all(out, "ma", 0, 0, tiled=True), rows))


def solution(mesh):
    placed = (
        P(("ma", "oct"), None, None),
        P("oct"),
        P("ma", "oct", None),
        P("ma", "oct", None),
        P("ma"),
        P(),
    )
    return jax.shard_map(
        on_device,
        mesh=mesh,
        in_specs=placed,
        out_specs=(P(("ma", "oct"), None, None), P(("ma", "oct"), None, None)),
        check_vma=False,
    )
```

```python
import functools

import jax
import jax.numpy as jnp
from jax import lax
from jax.experimental import pallas as pl
from jax.experimental.pallas import tpu as pltpu
from jax.sharding import PartitionSpec as P

LMAX = 2559
TILE = 128
SURE = (11, 5)
SHARED = 5
KEPT = SURE[0] + SHARED + SURE[1]
CUT = (SURE[0] + SHARED - 1) * TILE
SENT = (KEPT - 1) * TILE
HALF, ALL_FIRST, LANE, AT, AT_SENT = range(2 * SHARED, 2 * SHARED + 5)
BLOCK = 512
BF16 = jnp.bfloat16
F32 = jnp.float32
LIMIT = 32 * 1024 * 1024
IN_VMEM = pl.BlockSpec(memory_space=pltpu.VMEM)
IN_SMEM = pl.BlockSpec(memory_space=pltpu.SMEM)
IN_PLACE = pl.BlockSpec(memory_space=pl.ANY)
NN = ((1,), (0,))
TN = ((0,), (0,))
NT = ((1,), (1,))


def dot(a, b, dims):
    return lax.dot_general(a, b, (dims, ((), ())), preferred_element_type=F32)


def call(kernel, name, **kwargs):
    return pl.pallas_call(
        kernel, name=name, compiler_params=pltpu.CompilerParams(vmem_limit_bytes=LIMIT), **kwargs)


def fill_order(order, source):
    size = order.shape[0]
    index = source(lax.broadcasted_iota(jnp.int32, (size, 1), 0))
    hit = index == lax.broadcasted_iota(jnp.int32, (size, size), 1)
    order[...] = jnp.where(hit, 1.0, 0.0).astype(BF16)


def log2(n):
    return n.bit_length() - 1


def pack_kernel(wind_ref, out_ref, order8, order4):
    rows, slots, lanes = wind_ref.shape

    @pl.when(pl.program_id(0) == 0)
    def _():
        for count, order in ((8, order8), (4, order4)):
            c = log2(count)
            fill_order(order, lambda i: (i & (count - 1)) * slots + ((i >> (c + 1)) << 1) + ((i >> c) & 1))

    eights = []
    for start in (0, 8, 16):
        count, order = (8, order8) if start < 16 else (4, order4)
        block = wind_ref[start:start + count].reshape(count * slots, lanes)
        eights.append(dot(order[...], block, NN).reshape(slots // 2, 2 * count, lanes))
    for slot in range(2):
        rows_of = [x[:, 8 * slot:8 * slot + 8] for x in eights[:2]]
        out_ref[:, 16 * slot:16 * slot + 16] = jnp.concatenate(rows_of, axis=1).astype(BF16)
    out_ref[:, 32:] = eights[2].astype(BF16)


def pack(wind):
    rows, slots, width = wind.shape
    lanes = width // 2
    return call(
        pack_kernel,
        "pack",
        grid=(2,),
        out_shape=pltpu.HBM((slots // 2, rows * 2, width), BF16),
        in_specs=[pl.BlockSpec((rows, slots, lanes), lambda i: (0, 0, i))],
        out_specs=pl.BlockSpec((slots // 2, rows * 2, lanes), lambda i: (0, 0, i)),
        scratch_shapes=[
            pltpu.VMEM((8 * slots, 8 * slots), BF16),
            pltpu.VMEM((4 * slots, 4 * slots), BF16),
        ],
    )(*in_hbm(wind))


def unpack_kernel(payload, rot_ref, div_ref, outs, order8, order4, sems):
    _, rows, slots, width = outs.shape
    lanes = width // 4
    for count, order in ((8, order8), (4, order4)):
        c = log2(count)

        def source(i):
            slot = i & (slots - 1)
            return ((slot >> 1) << (c + 1)) + ((slot & 1) << c) + (i >> log2(slots))

        fill_order(order, source)
    copies = []
    for n, component in enumerate((0, 3, 1, 2)):
        cols = slice(2 * n * lanes, 2 * (n + 1) * lanes)
        mains = [payload[:, 16 * slot:16 * slot + 16, cols].astype(F32) for slot in range(2)]
        for start in (0, 8, 16):
            if start < 16:
                block = jnp.concatenate([x[:, start:start + 8] for x in mains], axis=1)
                count, order = 8, order8
            else:
                block = payload[:, 32:, cols].astype(F32)
                count, order = 4, order4
            moved = dot(order[...], block.reshape(count * slots, 2 * lanes).astype(BF16), NN)
            moved = moved.reshape(count, slots, 2 * lanes).astype(BF16)
            for k, ref in enumerate((rot_ref, div_ref)):
                outs[k, start:start + count, :, component * lanes:(component + 1) * lanes] = (
                    moved[:, :, k * lanes:(k + 1) * lanes])
                at = (pl.ds(start, count), slice(None), pl.ds(component * lanes, lanes))
                copies.append(pltpu.make_async_copy(outs.at[(k, *at)], ref.at[at], sems.at[len(copies)]))
                copies[-1].start()
    for copy in copies:
        copy.wait()


def unpack(payload, rows):
    pairs, both, width = payload.shape
    slots = pairs * 2
    shape = (rows, slots, width // 2)
    return call(
        unpack_kernel,
        "unpack",
        out_shape=(pltpu.HBM(shape, BF16), pltpu.HBM(shape, BF16)),
        in_specs=[IN_VMEM],
        out_specs=(IN_PLACE, IN_PLACE),
        scratch_shapes=[
            pltpu.VMEM((2, *shape), BF16),
            pltpu.VMEM((8 * slots, 8 * slots), BF16),
            pltpu.VMEM((4 * slots, 4 * slots), BF16),
            pltpu.SemaphoreType.DMA((24,)),
        ],
    )(payload)


def in_hbm(*arrays):
    return [pltpu.with_memory_space_constraint(x, pltpu.HBM) for x in arrays]


def keep_kernel(meta, p_ref, h_ref, out_ref, kept, sems, out_sems):
    quarter, degrees = p_ref.shape[1:]
    pieces = [(0, degrees - SURE[0] * TILE, SURE[0], 0)]
    for k in range(SHARED):
        pieces.append((meta[k], pl.multiple_of(meta[SHARED + k] * TILE, TILE), 1, SURE[0] + k))
    pieces.append((1, degrees - SURE[1] * TILE, SURE[1], SURE[0] + SHARED))
    copies = []
    for at, ref in enumerate((p_ref, h_ref)):
        for slot, source, count, target in pieces:
            copies.append(pltpu.make_async_copy(
                ref.at[slot, :, pl.ds(source, count * TILE)],
                kept.at[pl.ds(at * quarter, quarter), pl.ds(target * TILE, count * TILE)],
                sems.at[len(copies)],
            ))
            copies[-1].start()
    sent = []
    for at in range(2):
        for copy in copies[at * len(pieces):(at + 1) * len(pieces)]:
            copy.wait()
        rows = pl.ds(at * quarter, quarter)
        sent.append(pltpu.make_async_copy(kept.at[rows], out_ref.at[rows], out_sems.at[at]))
        sent[at].start()
    for copy in sent:
        copy.wait()


def keep(meta, p_table, h_table):
    shape = (2 * p_table.shape[1], KEPT * TILE)
    return call(
        keep_kernel,
        "keep",
        out_shape=pltpu.HBM(shape, BF16),
        in_specs=[IN_SMEM] + [IN_PLACE] * 2,
        out_specs=IN_PLACE,
        scratch_shapes=[
            pltpu.VMEM(shape, BF16),
            pltpu.SemaphoreType.DMA((2 * (2 + SHARED),)),
            pltpu.SemaphoreType.DMA((2,)),
        ],
    )(meta, *in_hbm(p_table, h_table))


STREAM = 512
N_BLOCKS = -(-KEPT * TILE // STREAM)


def forward_kernel(part, meta, rate, mask, weight, recv, select, table, factor, keep, send, *refs):
    del factor
    owners, both, width = recv.shape
    source, (table, wind, spec, sems) = table, refs
    copies = []
    for n in range(N_BLOCKS):
        cols = pl.ds(n * STREAM, min(STREAM, KEPT * TILE - n * STREAM))
        copies.append(pltpu.make_async_copy(source.at[:, cols], table.at[:, cols], sems.at[n]))
        copies[n].start()
    waited = 0
    quarter = select.shape[2]
    levels = width // 4
    main = owners * 16
    columns = [slice(at * levels, (at + 1) * levels) for at in (part, 3 - part)]
    mixed = [recv[:, 32:, cols].astype(F32).reshape(owners * 8, levels).astype(BF16) for cols in columns]
    for slot in range(2):
        rows = [recv[:, 16 * slot:16 * slot + 16, cols].reshape(main, levels) for cols in columns]
        by_lat = dot(jnp.concatenate(rows, axis=1), select[slot, :main], TN)
        by_lat = by_lat + dot(jnp.concatenate(mixed, axis=1), select[slot, main:], TN)
        wind[slot] = (by_lat * weight[...]).astype(BF16)
    split = (SURE[0] + SHARED) * TILE
    for slot in range(2):
        low, high = (0, split) if slot == 0 else (SURE[0] * TILE, KEPT * TILE)
        r = rate[slot]
        w = wind[slot]
        for start in range(low, high, BLOCK):
            cols = slice(start, min(start + BLOCK, high))
            while waited < len(copies) and waited * STREAM < cols.stop:
                copies[waited].wait()
                waited += 1
            proj_p = dot(w, table[:quarter, cols], NN)
            proj_h = dot(w, table[quarter:, cols], NN)
            psi = proj_h[:levels] - r * proj_p[levels:]
            chi = r * proj_p[:levels] - proj_h[levels:]
            if slot == 1 and start < split:
                first = mask[:, cols] > 0.5
                psi = jnp.where(first, spec[:levels, cols], psi)
                chi = jnp.where(first, spec[levels:, cols], chi)
            spec[:levels, cols] = psi
            spec[levels:, cols] = chi
    lane = lax.broadcasted_iota(jnp.int32, (2 * levels, TILE), 1)
    at = pl.ds(pl.multiple_of(meta[AT] * TILE, TILE), TILE)
    last, other = spec[:, CUT:CUT + TILE], spec[:, at]
    all_first = meta[ALL_FIRST] == 1
    low_first, low_second = jnp.where(all_first, last, other), jnp.where(all_first, other, last)
    spec[:, at] = jnp.where(lane >= meta[LANE], low_first, pltpu.roll(low_second, meta[LANE], 1))
    mine = pl.multiple_of(meta[HALF] * levels, levels)
    for ref, start in ((keep, mine), (send, levels - mine)):
        rows = pl.ds(pl.multiple_of(start, levels), levels)
        ref[:, :CUT] = spec[rows, :CUT].astype(ref.dtype)
        ref[:, CUT:] = spec[rows, CUT + TILE:].astype(ref.dtype)


def forward(part, meta, rate, mask, weight, recv, select, table, factor):
    owners, both, width = recv.shape
    levels = width // 4
    quarter = select.shape[2]
    out_shape = [jax.ShapeDtypeStruct((levels, SENT), F32), jax.ShapeDtypeStruct((levels, SENT), BF16)]
    scratch = [
        pltpu.VMEM((2, 2 * levels, quarter), BF16),
        pltpu.VMEM((2 * levels, KEPT * TILE), F32),
        pltpu.SemaphoreType.DMA((N_BLOCKS,)),
    ]
    (scratch, out_shape)[part].insert((0, 2)[part], pltpu.VMEM(table.shape, BF16))
    return call(
        functools.partial(forward_kernel, part),
        "forward",
        in_specs=[IN_SMEM] * 2 + [IN_VMEM] * 4 + [IN_PLACE] * 2,
        out_specs=[IN_VMEM] * len(out_shape),
        out_shape=out_shape,
        scratch_shapes=scratch,
        cost_estimate=pl.CostEstimate(flops=5 * 10**9, bytes_accessed=10**7, transcendentals=0),
    )(meta, rate, mask, weight, recv, select, *in_hbm(table), factor)


def backward_kernel(part, meta, rate, mask, mine, theirs, select, table, *refs):
    out_ref, every, masked, winds, out, sems = refs[-6:]
    levels = mine.shape[0]
    quarter = select.shape[2]
    owners, both, width = out.shape
    main = owners * 16
    split = (SURE[0] + SHARED) * TILE
    degrees = KEPT * TILE
    at = meta[HALF] * levels
    every[pl.ds(pl.multiple_of(at, levels), levels), :] = mine[...]
    every[pl.ds(pl.multiple_of(levels - at, levels), levels), :] = theirs[...]
    shared = slice(SURE[0] * TILE, split)
    cut = CUT - shared.start
    first = mask[:, shared.start:CUT] > 0.5
    both_slots = every[:, shared.start:CUT].astype(F32)
    lane = lax.broadcasted_iota(jnp.int32, (2 * levels, TILE), 1)
    joint = every[:, pl.ds(pl.multiple_of(meta[AT_SENT] * TILE, TILE), TILE)].astype(F32)
    back = TILE - meta[LANE]
    low_first = jnp.where(lane >= meta[LANE], joint, 0.0).astype(BF16)
    low_second = jnp.where(lane >= back, pltpu.roll(joint, back & (TILE - 1), 1), 0.0).astype(BF16)
    masked[0, :, :shared.start] = every[:, :shared.start]
    masked[0, :, shared.start:CUT] = jnp.where(first, both_slots, 0.0).astype(BF16)
    masked[1, :, :cut] = jnp.where(first, 0.0, both_slots).astype(BF16)
    masked[1, :, cut + TILE:degrees - shared.start] = every[:, CUT:]

    @pl.when(meta[ALL_FIRST] == 1)
    def _():
        masked[0, :, CUT:split] = low_first
        masked[1, :, cut:cut + TILE] = jnp.zeros_like(low_second)
        masked[1, :, cut + TILE:cut + 2 * TILE] = low_second

    @pl.when(meta[ALL_FIRST] != 1)
    def _():
        masked[0, :, CUT:split] = jnp.zeros_like(low_first)
        masked[0, :, pl.ds(pl.multiple_of(meta[AT] * TILE, TILE), TILE)] = low_first
        masked[1, :, cut:cut + TILE] = low_second

    for slot in range(2):
        low, high = (0, split) if slot == 0 else (shared.start, degrees)
        pot = masked[slot, :, :high - low]
        sums = [dot(table[n * quarter:(n + 1) * quarter, low:high], pot, NT) for n in range(2)]
        r = rate[slot]
        winds[slot, :, :levels] = (-sums[1][:, :levels]).astype(BF16)
        winds[slot, :, levels:2 * levels] = (-r * sums[0][:, levels:]).astype(BF16)
        winds[slot, :, 2 * levels:3 * levels] = (r * sums[0][:, :levels]).astype(BF16)
        winds[slot, :, 3 * levels:] = sums[1][:, levels:].astype(BF16)
    copies = []
    for n in range(2):
        cols = slice(n * width // 2, (n + 1) * width // 2)
        for slot in range(2):
            moved = dot(select[slot, :main], winds[slot, :, cols], NN)
            out[:, 16 * slot:16 * slot + 16, cols] = moved.astype(BF16).reshape(owners, 16, width // 2)
        mixed = dot(select[0, main:], winds[0, :, cols], NN) + dot(select[1, main:], winds[1, :, cols], NN)
        out[:, 32:, cols] = mixed.reshape(owners, 8, width // 2).astype(BF16)
        copies.append(pltpu.make_async_copy(
            out.at[:, :, pl.ds(n * width // 2, width // 2)],
            out_ref.at[:, :, pl.ds(part * width + n * width // 2, width // 2)],
            sems.at[n],
        ))
        copies[n].start()
    for copy in copies:
        copy.wait()


def backward(part, meta, rate, mask, mine, theirs, select, table, payload, filled=()):
    quarter = select.shape[2]
    levels = mine.shape[0]
    owners, both, width = payload
    piece = (owners, both, width // 2)
    return call(
        functools.partial(backward_kernel, part),
        "backward",
        in_specs=[IN_SMEM] * 2 + [IN_VMEM] * 5 + [IN_PLACE] * len(filled),
        out_specs=IN_PLACE,
        out_shape=pltpu.HBM(payload, BF16),
        input_output_aliases={7: 0} if filled else {},
        scratch_shapes=[
            pltpu.VMEM((2 * levels, SENT), BF16),
            pltpu.VMEM((2, 2 * levels, (SURE[0] + SHARED) * TILE), BF16),
            pltpu.VMEM((2, quarter, width // 2), BF16),
            pltpu.VMEM(piece, BF16),
            pltpu.SemaphoreType.DMA((2,)),
        ],
    )(meta, rate, mask, mine, theirs, select, table, *filled)


def add_kernel(kept, got, total, sent):
    total[...] = kept[...] + got[...].astype(F32)
    sent[...] = total[...].astype(BF16)


def add(kept, got):
    return call(
        add_kernel,
        "add",
        in_specs=[IN_VMEM] * 2,
        out_specs=[IN_VMEM] * 2,
        out_shape=[jax.ShapeDtypeStruct(kept.shape, F32), jax.ShapeDtypeStruct(kept.shape, BF16)],
    )(kept, got)


def scale_kernel(kept, got, factor, mine):
    mine[...] = ((kept[...] + got[...].astype(F32)) * factor[...]).astype(BF16)


def scale(kept, got, factor):
    return call(
        scale_kernel,
        "scale",
        in_specs=[IN_VMEM] * 3,
        out_specs=IN_VMEM,
        out_shape=jax.ShapeDtypeStruct(kept.shape, BF16),
    )(kept, got, factor)


def layout(wavenumbers, count, half):
    low_first, low_second = wavenumbers[0] // TILE, wavenumbers[1] // TILE
    n_first = count - low_first - SURE[0]
    k = jnp.arange(SHARED)
    shared_slot = (k >= n_first).astype(jnp.int32)
    shared_tile = jnp.where(k < n_first, count - SURE[0] - 1 - k, count - SURE[1] - 1 - (k - n_first))
    slot = jnp.concatenate([jnp.zeros(SURE[0], jnp.int32), shared_slot, jnp.ones(SURE[1], jnp.int32)])
    mask = jnp.repeat(1.0 - slot.astype(F32), TILE)[None, :]
    all_first = n_first == SHARED
    at = jnp.where(n_first == 0, 0, SURE[0] - 1 + n_first)
    at, at_sent = jnp.where(all_first, SURE[0] + SHARED, at), jnp.where(all_first, SURE[0] + SHARED - 1, at)
    lane_first = wavenumbers[0] % TILE
    scalars = jnp.stack([half, all_first.astype(jnp.int32), lane_first, at, at_sent])
    meta = jnp.concatenate([shared_slot, shared_tile, scalars]).astype(jnp.int32)
    tile = jnp.concatenate([jnp.arange(count - SURE[0], count), shared_tile[:-1], jnp.arange(count - SURE[1], count)])
    joint = jnp.arange(tile.shape[0]) == at_sent
    lane = jnp.arange(TILE)
    degree = jnp.where(joint, low_first, tile)[:, None] * TILE + lane[None, :]
    degree_second = low_second * TILE + TILE + lane - lane_first
    degree = jnp.where(joint[:, None] & (lane < lane_first)[None, :], degree_second[None, :], degree).astype(F32)
    factor = (-(LMAX * LMAX * 1.0) / jnp.maximum(degree * (degree + 1.0), 1.0)).reshape(1, -1)
    return meta, mask, factor


def on_device(fourier_wind, quad_weight, p_table, h_table, wavenumbers, row_latitude):
    owners = lax.axis_size("ma")
    groups = lax.axis_size("oct")
    me = lax.axis_index("oct")
    rows = fourier_wind.shape[0]
    quarter = p_table.shape[1]
    count = p_table.shape[2] // TILE
    flip, turn = [z ^ 1 for z in range(groups)], [groups - 1 - z for z in range(groups)]
    first = [
        (d * groups + z, d * groups + (flip, turn)[d % 2][z]) for d in range(owners) for z in range(groups)]
    second = [
        (d * groups + z, d * groups + (turn, flip)[d % 2][z]) for d in range(owners) for z in range(groups)]
    half = jnp.where(lax.axis_index("ma") % 2 == 0, ((me + 1) // 2) % 2, me // 2)

    def swap(x, pairs):
        return lax.ppermute(x, ("ma", "oct"), pairs)

    received = lax.all_to_all(pack(fourier_wind), "ma", 0, 0, tiled=True)

    meta, mask, factor = layout(wavenumbers, count, half)
    rate = wavenumbers.astype(F32) / LMAX

    local = lax.dynamic_index_in_dim(row_latitude.reshape(owners, groups, rows), me, 1, keepdims=False) - me * quarter
    none = jnp.full((owners, 4), -1, jnp.int32)
    main, last = local[:, :16].reshape(-1), local[:, 16:]
    target = jnp.stack([
        jnp.concatenate([main, jnp.concatenate([last, none], axis=1).reshape(-1)]),
        jnp.concatenate([main, jnp.concatenate([none, last], axis=1).reshape(-1)]),
    ])
    select = (target[:, :, None] == jnp.arange(quarter)[None, None, :]).astype(BF16)
    weight = quad_weight.reshape(1, -1)

    table = keep(meta, p_table, h_table)
    owners, both, width = received.shape
    payload = (owners, both, 2 * width)
    signs = (rate, -rate)
    kept_a, sent_a = forward(0, meta, signs[0], mask, weight, received, select, table, factor)
    kept_b, sent_b, table = forward(1, meta, signs[1], mask, weight, received, select, table, factor)
    table = pltpu.with_memory_space_constraint(table, pltpu.VMEM)
    kept_a, sent_a = add(kept_a, swap(sent_a, first))
    kept_b, sent_b = add(kept_b, swap(sent_b, first))
    mine_a = scale(kept_a, swap(sent_a, second), factor)
    mine_b = scale(kept_b, swap(sent_b, second), factor)
    out = backward(0, meta, signs[0], mask, mine_a, swap(mine_a, first), select, table, payload)
    out = backward(1, meta, signs[1], mask, mine_b, swap(mine_b, first), select, table, payload, (out,))
    return tuple(unpack(lax.all_to_all(out, "ma", 0, 0, tiled=True), rows))


def solution(mesh):
    placed = (
        P(("ma", "oct"), None, None),
        P("oct"),
        P("ma", "oct", None),
        P("ma", "oct", None),
        P("ma"),
        P(),
    )
    return jax.shard_map(
        on_device,
        mesh=mesh,
        in_specs=placed,
        out_specs=(P(("ma", "oct"), None, None), P(("ma", "oct"), None, None)),
        check_vma=False,
    )
```

```python
import functools

import jax
import jax.numpy as jnp
from jax import lax
from jax.experimental import pallas as pl
from jax.experimental.pallas import tpu as pltpu
from jax.sharding import PartitionSpec as P

LMAX = 2559
TILE = 128
SURE = (11, 5)
SHARED = 5
KEPT = SURE[0] + SHARED + SURE[1]
CUT = (SURE[0] + SHARED - 1) * TILE
SENT = (KEPT - 1) * TILE
HALF, ALL_FIRST, LANE, AT, AT_SENT = range(2 * SHARED, 2 * SHARED + 5)
BLOCK = 512
STREAM = 512
N_BLOCKS = -(-KEPT * TILE // STREAM)
BF16 = jnp.bfloat16
F32 = jnp.float32
LIMIT = 32 * 1024 * 1024
IN_VMEM = pl.BlockSpec(memory_space=pltpu.VMEM)
IN_SMEM = pl.BlockSpec(memory_space=pltpu.SMEM)
IN_PLACE = pl.BlockSpec(memory_space=pl.ANY)
NN = ((1,), (0,))
TN = ((0,), (0,))
NT = ((1,), (1,))


def dot(a, b, dims):
    return lax.dot_general(a, b, (dims, ((), ())), preferred_element_type=F32)


def call(kernel, name, **kwargs):
    return pl.pallas_call(
        kernel, name=name, compiler_params=pltpu.CompilerParams(vmem_limit_bytes=LIMIT), **kwargs)


def fill_order(order, source):
    size = order.shape[0]
    index = source(lax.broadcasted_iota(jnp.int32, (size, 1), 0))
    hit = index == lax.broadcasted_iota(jnp.int32, (size, size), 1)
    order[...] = jnp.where(hit, 1.0, 0.0).astype(BF16)


def log2(n):
    return n.bit_length() - 1


def pack_kernel(wind_ref, out_ref, order8, order4):
    rows, slots, lanes = wind_ref.shape

    @pl.when(pl.program_id(0) == 0)
    def _():
        for count, order in ((8, order8), (4, order4)):
            c = log2(count)
            fill_order(order, lambda i: (i & (count - 1)) * slots + ((i >> (c + 1)) << 1) + ((i >> c) & 1))

    eights = []
    for start in (0, 8, 16):
        count, order = (8, order8) if start < 16 else (4, order4)
        block = wind_ref[start:start + count].reshape(count * slots, lanes)
        eights.append(dot(order[...], block, NN).reshape(slots // 2, 2 * count, lanes))
    for slot in range(2):
        rows_of = [x[:, 8 * slot:8 * slot + 8] for x in eights[:2]]
        out_ref[:, 16 * slot:16 * slot + 16] = jnp.concatenate(rows_of, axis=1).astype(BF16)
    out_ref[:, 32:] = eights[2].astype(BF16)


def pack(wind):
    rows, slots, width = wind.shape
    lanes = width // 2
    return call(
        pack_kernel,
        "pack",
        grid=(2,),
        out_shape=pltpu.HBM((slots // 2, rows * 2, width), BF16),
        in_specs=[pl.BlockSpec((rows, slots, lanes), lambda i: (0, 0, i))],
        out_specs=pl.BlockSpec((slots // 2, rows * 2, lanes), lambda i: (0, 0, i)),
        scratch_shapes=[
            pltpu.VMEM((8 * slots, 8 * slots), BF16),
            pltpu.VMEM((4 * slots, 4 * slots), BF16),
        ],
    )(*in_hbm(wind))


def unpack_kernel(payload, rot_ref, div_ref, outs, order8, order4, sems):
    _, rows, slots, width = outs.shape
    lanes = width // 4
    for count, order in ((8, order8), (4, order4)):
        c = log2(count)

        def source(i):
            slot = i & (slots - 1)
            return ((slot >> 1) << (c + 1)) + ((slot & 1) << c) + (i >> log2(slots))

        fill_order(order, source)
    copies = []
    for n, component in enumerate((0, 3, 1, 2)):
        cols = slice(2 * n * lanes, 2 * (n + 1) * lanes)
        mains = [payload[:, 16 * slot:16 * slot + 16, cols].astype(F32) for slot in range(2)]
        for start in (0, 8, 16):
            if start < 16:
                block = jnp.concatenate([x[:, start:start + 8] for x in mains], axis=1)
                count, order = 8, order8
            else:
                block = payload[:, 32:, cols].astype(F32)
                count, order = 4, order4
            moved = dot(order[...], block.reshape(count * slots, 2 * lanes).astype(BF16), NN)
            moved = moved.reshape(count, slots, 2 * lanes).astype(BF16)
            for k, ref in enumerate((rot_ref, div_ref)):
                outs[k, start:start + count, :, component * lanes:(component + 1) * lanes] = (
                    moved[:, :, k * lanes:(k + 1) * lanes])
                at = (pl.ds(start, count), slice(None), pl.ds(component * lanes, lanes))
                copies.append(pltpu.make_async_copy(outs.at[(k, *at)], ref.at[at], sems.at[len(copies)]))
                copies[-1].start()
    for copy in copies:
        copy.wait()


def unpack(payload, rows):
    pairs, both, width = payload.shape
    slots = pairs * 2
    shape = (rows, slots, width // 2)
    return call(
        unpack_kernel,
        "unpack",
        out_shape=(pltpu.HBM(shape, BF16), pltpu.HBM(shape, BF16)),
        in_specs=[IN_VMEM],
        out_specs=(IN_PLACE, IN_PLACE),
        scratch_shapes=[
            pltpu.VMEM((2, *shape), BF16),
            pltpu.VMEM((8 * slots, 8 * slots), BF16),
            pltpu.VMEM((4 * slots, 4 * slots), BF16),
            pltpu.SemaphoreType.DMA((24,)),
        ],
    )(payload)


def in_hbm(*arrays):
    return [pltpu.with_memory_space_constraint(x, pltpu.HBM) for x in arrays]


def keep_kernel(meta, select, p_ref, h_ref, out_ref, kept, moved, sems, out_sems):
    quarter, degrees = p_ref.shape[1:]
    pieces = [(0, degrees - SURE[0] * TILE, SURE[0], 0)]
    for k in range(SHARED):
        pieces.append((meta[k], pl.multiple_of(meta[SHARED + k] * TILE, TILE), 1, SURE[0] + k))
    pieces.append((1, degrees - SURE[1] * TILE, SURE[1], SURE[0] + SHARED))
    copies = []
    for at, ref in enumerate((p_ref, h_ref)):
        for slot, source, count, target in pieces:
            copies.append(pltpu.make_async_copy(
                ref.at[slot, :, pl.ds(source, count * TILE)],
                kept.at[pl.ds(at * quarter, quarter), pl.ds(target * TILE, count * TILE)],
                sems.at[len(copies)],
            ))
            copies[-1].start()
    sent = []
    for at in range(2):
        for copy in copies[at * len(pieces):(at + 1) * len(pieces)]:
            copy.wait()
        rows = slice(at * quarter, (at + 1) * quarter)
        for n in range(N_BLOCKS):
            start, size = n * STREAM, min(STREAM, KEPT * TILE - n * STREAM)
            cols = slice(start, start + size)
            moved[rows, cols] = dot(select[...], kept[rows, cols], NN).astype(BF16)
            block = (pl.ds(at * quarter, quarter), pl.ds(start, size))
            sent.append(pltpu.make_async_copy(moved.at[block], out_ref.at[block], out_sems.at[len(sent)]))
            sent[-1].start()
    for copy in sent:
        copy.wait()


def keep(meta, select, p_table, h_table):
    shape = (2 * p_table.shape[1], KEPT * TILE)
    return call(
        keep_kernel,
        "keep",
        out_shape=pltpu.HBM(shape, BF16),
        in_specs=[IN_SMEM, IN_VMEM] + [IN_PLACE] * 2,
        out_specs=IN_PLACE,
        scratch_shapes=[
            pltpu.VMEM(shape, BF16),
            pltpu.VMEM(shape, BF16),
            pltpu.SemaphoreType.DMA((2 * (2 + SHARED),)),
            pltpu.SemaphoreType.DMA((2 * N_BLOCKS,)),
        ],
    )(meta, select, *in_hbm(p_table, h_table))


def last_rows(slot, owners):
    i = lax.broadcasted_iota(jnp.int32, (4 * owners, 1), 0)
    hit = ((i >> 2) << 3) + (i & 3) + 4 * slot == lax.broadcasted_iota(jnp.int32, (4 * owners, 8 * owners), 1)
    return jnp.where(hit, 1.0, 0.0).astype(BF16)


def forward_kernel(part, meta, rate, mask, weight, recv, table, factor, keep, send, *refs):
    del factor
    owners, both, width = recv.shape
    source, (table, wind, spec, sems) = table, refs
    copies = []
    for n in range(N_BLOCKS):
        cols = pl.ds(n * STREAM, min(STREAM, KEPT * TILE - n * STREAM))
        copies.append(pltpu.make_async_copy(source.at[:, cols], table.at[:, cols], sems.at[n]))
        copies[n].start()
    waited = 0
    quarter = weight.shape[0]
    levels = width // 4
    main = owners * 16
    columns = [slice(at * levels, (at + 1) * levels) for at in (part, 3 - part)]
    mixed = [recv[:, 32:, cols].astype(F32).reshape(owners * 8, levels).astype(BF16) for cols in columns]
    mixed = jnp.concatenate(mixed, axis=1)
    for slot in range(2):
        rows = [recv[:, 16 * slot:16 * slot + 16, cols].reshape(main, levels).astype(F32) for cols in columns]
        rows = [jnp.concatenate(rows, axis=1), dot(last_rows(slot, owners), mixed, NN)]
        weighted = jnp.concatenate(rows, axis=0) * weight[...]
        wind[slot] = weighted.T.astype(BF16)
    split = (SURE[0] + SHARED) * TILE
    for slot in range(2):
        low, high = (0, split) if slot == 0 else (SURE[0] * TILE, KEPT * TILE)
        r = rate[slot]
        w = wind[slot]
        for start in range(low, high, BLOCK):
            cols = slice(start, min(start + BLOCK, high))
            while waited < len(copies) and waited * STREAM < cols.stop:
                copies[waited].wait()
                waited += 1
            proj_p = dot(w, table[:quarter, cols], NN)
            proj_h = dot(w, table[quarter:, cols], NN)
            psi = proj_h[:levels] - r * proj_p[levels:]
            chi = r * proj_p[:levels] - proj_h[levels:]
            if slot == 1 and start < split:
                first = mask[:, cols] > 0.5
                psi = jnp.where(first, spec[:levels, cols], psi)
                chi = jnp.where(first, spec[levels:, cols], chi)
            spec[:levels, cols] = psi
            spec[levels:, cols] = chi
    lane = lax.broadcasted_iota(jnp.int32, (2 * levels, TILE), 1)
    at = pl.ds(pl.multiple_of(meta[AT] * TILE, TILE), TILE)
    last, other = spec[:, CUT:CUT + TILE], spec[:, at]
    all_first = meta[ALL_FIRST] == 1
    low_first, low_second = jnp.where(all_first, last, other), jnp.where(all_first, other, last)
    spec[:, at] = jnp.where(lane >= meta[LANE], low_first, pltpu.roll(low_second, meta[LANE], 1))
    mine = pl.multiple_of(meta[HALF] * levels, levels)
    for ref, start in ((keep, mine), (send, levels - mine)):
        rows = pl.ds(pl.multiple_of(start, levels), levels)
        ref[:, :CUT] = spec[rows, :CUT].astype(ref.dtype)
        ref[:, CUT:] = spec[rows, CUT + TILE:].astype(ref.dtype)


def forward(part, meta, rate, mask, weight, recv, table, factor):
    owners, both, width = recv.shape
    levels = width // 4
    quarter = weight.shape[0]
    out_shape = [jax.ShapeDtypeStruct((levels, SENT), F32), jax.ShapeDtypeStruct((levels, SENT), BF16)]
    scratch = [
        pltpu.VMEM((2, 2 * levels, quarter), BF16),
        pltpu.VMEM((2 * levels, KEPT * TILE), F32),
        pltpu.SemaphoreType.DMA((N_BLOCKS,)),
    ]
    (scratch, out_shape)[part].insert((0, 2)[part], pltpu.VMEM(table.shape, BF16))
    return call(
        functools.partial(forward_kernel, part),
        "forward",
        in_specs=[IN_SMEM] * 2 + [IN_VMEM] * 3 + [IN_PLACE] * 2,
        out_specs=[IN_VMEM] * len(out_shape),
        out_shape=out_shape,
        scratch_shapes=scratch,
        cost_estimate=pl.CostEstimate(flops=5 * 10**9, bytes_accessed=10**7, transcendentals=0),
    )(meta, rate, mask, weight, recv, *in_hbm(table), factor)


def backward_kernel(part, meta, rate, mask, mine, theirs, table, *refs):
    out_ref, every, masked, last, out, sems = refs[-6:]
    levels = mine.shape[0]
    quarter = table.shape[0] // 2
    owners, both, width = out.shape
    main = owners * 16
    split = (SURE[0] + SHARED) * TILE
    degrees = KEPT * TILE
    at = meta[HALF] * levels
    every[pl.ds(pl.multiple_of(at, levels), levels), :] = mine[...]
    every[pl.ds(pl.multiple_of(levels - at, levels), levels), :] = theirs[...]
    shared = slice(SURE[0] * TILE, split)
    cut = CUT - shared.start
    first = mask[:, shared.start:CUT] > 0.5
    both_slots = every[:, shared.start:CUT].astype(F32)
    lane = lax.broadcasted_iota(jnp.int32, (2 * levels, TILE), 1)
    joint = every[:, pl.ds(pl.multiple_of(meta[AT_SENT] * TILE, TILE), TILE)].astype(F32)
    back = TILE - meta[LANE]
    low_first = jnp.where(lane >= meta[LANE], joint, 0.0).astype(BF16)
    low_second = jnp.where(lane >= back, pltpu.roll(joint, back & (TILE - 1), 1), 0.0).astype(BF16)
    masked[0, :, :shared.start] = every[:, :shared.start]
    masked[0, :, shared.start:CUT] = jnp.where(first, both_slots, 0.0).astype(BF16)
    masked[1, :, :cut] = jnp.where(first, 0.0, both_slots).astype(BF16)
    masked[1, :, cut + TILE:degrees - shared.start] = every[:, CUT:]

    @pl.when(meta[ALL_FIRST] == 1)
    def _():
        masked[0, :, CUT:split] = low_first
        masked[1, :, cut:cut + TILE] = jnp.zeros_like(low_second)
        masked[1, :, cut + TILE:cut + 2 * TILE] = low_second

    @pl.when(meta[ALL_FIRST] != 1)
    def _():
        masked[0, :, CUT:split] = jnp.zeros_like(low_first)
        masked[0, :, pl.ds(pl.multiple_of(meta[AT] * TILE, TILE), TILE)] = low_first
        masked[1, :, cut:cut + TILE] = low_second

    for slot in range(2):
        low, high = (0, split) if slot == 0 else (shared.start, degrees)
        pot = masked[slot, :, :high - low]
        sums = [dot(table[n * quarter:(n + 1) * quarter, low:high], pot, NT) for n in range(2)]
        r = rate[slot]
        fields = (-sums[1][:, :levels], -r * sums[0][:, levels:], r * sums[0][:, :levels], sums[1][:, levels:])
        for n, field in enumerate(fields):
            field = field.astype(BF16)
            cols = slice(n * levels, (n + 1) * levels)
            out[:, 16 * slot:16 * slot + 16, cols] = field[:main].reshape(owners, 16, levels)
            last[slot, :, cols] = field[main:]
    mixed = dot(last_rows(0, owners), last[0], TN) + dot(last_rows(1, owners), last[1], TN)
    out[:, 32:] = mixed.reshape(owners, 8, width).astype(BF16)
    sent = []
    for n in range(4):
        some = owners // 4
        sent.append(pltpu.make_async_copy(
            out.at[pl.ds(n * some, some)],
            out_ref.at[pl.ds(n * some, some), :, pl.ds(part * width, width)],
            sems.at[n],
        ))
        sent[n].start()
    for copy in sent:
        copy.wait()


def backward(part, meta, rate, mask, mine, theirs, table, payload, filled=()):
    levels = mine.shape[0]
    owners, both, width = payload
    piece = (owners, both, width // 2)
    return call(
        functools.partial(backward_kernel, part),
        "backward",
        in_specs=[IN_SMEM] * 2 + [IN_VMEM] * 4 + [IN_PLACE] * len(filled),
        out_specs=IN_PLACE,
        out_shape=pltpu.HBM(payload, BF16),
        input_output_aliases={6: 0} if filled else {},
        scratch_shapes=[
            pltpu.VMEM((2 * levels, SENT), BF16),
            pltpu.VMEM((2, 2 * levels, (SURE[0] + SHARED) * TILE), BF16),
            pltpu.VMEM((2, owners * 4, width // 2), BF16),
            pltpu.VMEM(piece, BF16),
            pltpu.SemaphoreType.DMA((4,)),
        ],
    )(meta, rate, mask, mine, theirs, table, *filled)


def add_kernel(kept, got, total, sent):
    total[...] = kept[...] + got[...].astype(F32)
    sent[...] = total[...].astype(BF16)


def add(kept, got):
    return call(
        add_kernel,
        "add",
        in_specs=[IN_VMEM] * 2,
        out_specs=[IN_VMEM] * 2,
        out_shape=[jax.ShapeDtypeStruct(kept.shape, F32), jax.ShapeDtypeStruct(kept.shape, BF16)],
    )(kept, got)


def scale_kernel(kept, got, factor, mine):
    mine[...] = ((kept[...] + got[...].astype(F32)) * factor[...]).astype(BF16)


def scale(kept, got, factor):
    return call(
        scale_kernel,
        "scale",
        in_specs=[IN_VMEM] * 3,
        out_specs=IN_VMEM,
        out_shape=jax.ShapeDtypeStruct(kept.shape, BF16),
    )(kept, got, factor)


def layout(wavenumbers, count, half):
    low_first, low_second = wavenumbers[0] // TILE, wavenumbers[1] // TILE
    n_first = count - low_first - SURE[0]
    k = jnp.arange(SHARED)
    shared_slot = (k >= n_first).astype(jnp.int32)
    shared_tile = jnp.where(k < n_first, count - SURE[0] - 1 - k, count - SURE[1] - 1 - (k - n_first))
    slot = jnp.concatenate([jnp.zeros(SURE[0], jnp.int32), shared_slot, jnp.ones(SURE[1], jnp.int32)])
    mask = jnp.repeat(1.0 - slot.astype(F32), TILE)[None, :]
    all_first = n_first == SHARED
    at = jnp.where(n_first == 0, 0, SURE[0] - 1 + n_first)
    at, at_sent = jnp.where(all_first, SURE[0] + SHARED, at), jnp.where(all_first, SURE[0] + SHARED - 1, at)
    lane_first = wavenumbers[0] % TILE
    scalars = jnp.stack([half, all_first.astype(jnp.int32), lane_first, at, at_sent])
    meta = jnp.concatenate([shared_slot, shared_tile, scalars]).astype(jnp.int32)
    tile = jnp.concatenate([jnp.arange(count - SURE[0], count), shared_tile[:-1], jnp.arange(count - SURE[1], count)])
    joint = jnp.arange(tile.shape[0]) == at_sent
    lane = jnp.arange(TILE)
    degree = jnp.where(joint, low_first, tile)[:, None] * TILE + lane[None, :]
    degree_second = low_second * TILE + TILE + lane - lane_first
    degree = jnp.where(joint[:, None] & (lane < lane_first)[None, :], degree_second[None, :], degree).astype(F32)
    factor = (-(LMAX * LMAX * 1.0) / jnp.maximum(degree * (degree + 1.0), 1.0)).reshape(1, -1)
    return meta, mask, factor


def on_device(fourier_wind, quad_weight, p_table, h_table, wavenumbers, row_latitude):
    owners = lax.axis_size("ma")
    groups = lax.axis_size("oct")
    me = lax.axis_index("oct")
    rows = fourier_wind.shape[0]
    quarter = p_table.shape[1]
    count = p_table.shape[2] // TILE
    flip, turn = [z ^ 1 for z in range(groups)], [groups - 1 - z for z in range(groups)]
    first = [
        (d * groups + z, d * groups + (flip, turn)[d % 2][z]) for d in range(owners) for z in range(groups)]
    second = [
        (d * groups + z, d * groups + (turn, flip)[d % 2][z]) for d in range(owners) for z in range(groups)]
    half = jnp.where(lax.axis_index("ma") % 2 == 0, ((me + 1) // 2) % 2, me // 2)

    def swap(x, pairs):
        return lax.ppermute(x, ("ma", "oct"), pairs)

    received = lax.all_to_all(pack(fourier_wind), "ma", 0, 0, tiled=True)

    meta, mask, factor = layout(wavenumbers, count, half)
    rate = wavenumbers.astype(F32) / LMAX

    local = lax.dynamic_index_in_dim(row_latitude.reshape(owners, groups, rows), me, 1, keepdims=False) - me * quarter
    target = jnp.concatenate([local[:, :16].reshape(-1), local[:, 16:].reshape(-1)])[:, None]
    hit = target == jnp.arange(quarter)[None, :]
    weight = jnp.sum(jnp.where(hit, quad_weight[None, :], 0.0), axis=1, keepdims=True)
    table = keep(meta, hit.astype(BF16), p_table, h_table)
    owners, both, width = received.shape
    payload = (owners, both, 2 * width)
    signs = (rate, -rate)
    kept_a, sent_a = forward(0, meta, signs[0], mask, weight, received, table, factor)
    kept_b, sent_b, table = forward(1, meta, signs[1], mask, weight, received, table, factor)
    table = pltpu.with_memory_space_constraint(table, pltpu.VMEM)
    kept_a, sent_a = add(kept_a, swap(sent_a, first))
    kept_b, sent_b = add(kept_b, swap(sent_b, first))
    mine_a = scale(kept_a, swap(sent_a, second), factor)
    mine_b = scale(kept_b, swap(sent_b, second), factor)
    out = backward(0, meta, signs[0], mask, mine_a, swap(mine_a, first), table, payload)
    out = backward(1, meta, signs[1], mask, mine_b, swap(mine_b, first), table, payload, (out,))
    return tuple(unpack(lax.all_to_all(out, "ma", 0, 0, tiled=True), rows))


def solution(mesh):
    placed = (
        P(("ma", "oct"), None, None),
        P("oct"),
        P("ma", "oct", None),
        P("ma", "oct", None),
        P("ma"),
        P(),
    )
    return jax.shard_map(
        on_device,
        mesh=mesh,
        in_specs=placed,
        out_specs=(P(("ma", "oct"), None, None), P(("ma", "oct"), None, None)),
        check_vma=False,
    )
```

```python
import functools

import jax
import jax.numpy as jnp
from jax import lax
from jax.experimental import pallas as pl
from jax.experimental.pallas import tpu as pltpu
from jax.sharding import PartitionSpec as P

LMAX = 2559
TILE = 128
SURE = (11, 5)
SHARED = 5
KEPT = SURE[0] + SHARED + SURE[1]
CUT = (SURE[0] + SHARED - 1) * TILE
SENT = (KEPT - 1) * TILE
HALF, ALL_FIRST, LANE, AT, AT_SENT = range(2 * SHARED, 2 * SHARED + 5)
BLOCK = 512
STREAM = 512
N_BLOCKS = -(-KEPT * TILE // STREAM)
BF16 = jnp.bfloat16
F32 = jnp.float32
LIMIT = 32 * 1024 * 1024
IN_VMEM = pl.BlockSpec(memory_space=pltpu.VMEM)
IN_SMEM = pl.BlockSpec(memory_space=pltpu.SMEM)
IN_PLACE = pl.BlockSpec(memory_space=pl.ANY)
NN = ((1,), (0,))
TN = ((0,), (0,))
NT = ((1,), (1,))


def dot(a, b, dims):
    return lax.dot_general(a, b, (dims, ((), ())), preferred_element_type=F32)


def call(kernel, name, **kwargs):
    return pl.pallas_call(
        kernel, name=name, compiler_params=pltpu.CompilerParams(vmem_limit_bytes=LIMIT), **kwargs)


def fill_order(order, source):
    size = order.shape[0]
    index = source(lax.broadcasted_iota(jnp.int32, (size, 1), 0))
    hit = index == lax.broadcasted_iota(jnp.int32, (size, size), 1)
    order[...] = jnp.where(hit, 1.0, 0.0).astype(BF16)


def log2(n):
    return n.bit_length() - 1


def pack_kernel(wind_ref, out_ref, order8, order4):
    rows, slots, lanes = wind_ref.shape

    @pl.when(pl.program_id(0) == 0)
    def _():
        for count, order in ((8, order8), (4, order4)):
            c = log2(count)
            fill_order(order, lambda i: (i & (count - 1)) * slots + ((i >> (c + 1)) << 1) + ((i >> c) & 1))

    eights = []
    for start in (0, 8, 16):
        count, order = (8, order8) if start < 16 else (4, order4)
        block = wind_ref[start:start + count].reshape(count * slots, lanes)
        eights.append(dot(order[...], block, NN).reshape(slots // 2, 2 * count, lanes))
    for slot in range(2):
        rows_of = [x[:, 8 * slot:8 * slot + 8] for x in eights[:2]]
        out_ref[:, 16 * slot:16 * slot + 16] = jnp.concatenate(rows_of, axis=1).astype(BF16)
    out_ref[:, 32:] = eights[2].astype(BF16)


def pack(wind):
    rows, slots, width = wind.shape
    lanes = width // 2
    return call(
        pack_kernel,
        "pack",
        grid=(2,),
        out_shape=pltpu.HBM((slots // 2, rows * 2, width), BF16),
        in_specs=[pl.BlockSpec((rows, slots, lanes), lambda i: (0, 0, i))],
        out_specs=pl.BlockSpec((slots // 2, rows * 2, lanes), lambda i: (0, 0, i)),
        scratch_shapes=[
            pltpu.VMEM((8 * slots, 8 * slots), BF16),
            pltpu.VMEM((4 * slots, 4 * slots), BF16),
        ],
    )(*in_hbm(wind))


def unpack_kernel(payload, rot_ref, div_ref, outs, order8, order4, sems):
    _, rows, slots, width = outs.shape
    lanes = width // 4
    for count, order in ((8, order8), (4, order4)):
        c = log2(count)

        def source(i):
            slot = i & (slots - 1)
            return ((slot >> 1) << (c + 1)) + ((slot & 1) << c) + (i >> log2(slots))

        fill_order(order, source)
    copies = []
    for n, component in enumerate((0, 3, 1, 2)):
        cols = slice(2 * n * lanes, 2 * (n + 1) * lanes)
        mains = [payload[:, 16 * slot:16 * slot + 16, cols].astype(F32) for slot in range(2)]
        for start in (0, 8, 16):
            if start < 16:
                block = jnp.concatenate([x[:, start:start + 8] for x in mains], axis=1)
                count, order = 8, order8
            else:
                block = payload[:, 32:, cols].astype(F32)
                count, order = 4, order4
            moved = dot(order[...], block.reshape(count * slots, 2 * lanes).astype(BF16), NN)
            moved = moved.reshape(count, slots, 2 * lanes).astype(BF16)
            for k, ref in enumerate((rot_ref, div_ref)):
                outs[k, start:start + count, :, component * lanes:(component + 1) * lanes] = (
                    moved[:, :, k * lanes:(k + 1) * lanes])
                at = (pl.ds(start, count), slice(None), pl.ds(component * lanes, lanes))
                copies.append(pltpu.make_async_copy(outs.at[(k, *at)], ref.at[at], sems.at[len(copies)]))
                copies[-1].start()
    for copy in copies:
        copy.wait()


def unpack(payload, rows):
    pairs, both, width = payload.shape
    slots = pairs * 2
    shape = (rows, slots, width // 2)
    return call(
        unpack_kernel,
        "unpack",
        out_shape=(pltpu.HBM(shape, BF16), pltpu.HBM(shape, BF16)),
        in_specs=[IN_VMEM],
        out_specs=(IN_PLACE, IN_PLACE),
        scratch_shapes=[
            pltpu.VMEM((2, *shape), BF16),
            pltpu.VMEM((8 * slots, 8 * slots), BF16),
            pltpu.VMEM((4 * slots, 4 * slots), BF16),
            pltpu.SemaphoreType.DMA((24,)),
        ],
    )(payload)


def in_hbm(*arrays):
    return [pltpu.with_memory_space_constraint(x, pltpu.HBM) for x in arrays]


def keep_kernel(meta, select, p_ref, h_ref, out_ref, kept, moved, sems, out_sems):
    quarter, degrees = p_ref.shape[1:]
    pieces = [(0, degrees - SURE[0] * TILE, SURE[0], 0)]
    for k in range(SHARED):
        pieces.append((meta[k], pl.multiple_of(meta[SHARED + k] * TILE, TILE), 1, SURE[0] + k))
    pieces.append((1, degrees - SURE[1] * TILE, SURE[1], SURE[0] + SHARED))
    copies = []
    for at, ref in enumerate((p_ref, h_ref)):
        for slot, source, count, target in pieces:
            copies.append(pltpu.make_async_copy(
                ref.at[slot, :, pl.ds(source, count * TILE)],
                kept.at[pl.ds(at * quarter, quarter), pl.ds(target * TILE, count * TILE)],
                sems.at[len(copies)],
            ))
            copies[-1].start()
    sent = []
    for at in range(2):
        for copy in copies[at * len(pieces):(at + 1) * len(pieces)]:
            copy.wait()
        rows = slice(at * quarter, (at + 1) * quarter)
        for n in range(N_BLOCKS):
            start, size = n * STREAM, min(STREAM, KEPT * TILE - n * STREAM)
            cols = slice(start, start + size)
            moved[rows, cols] = dot(select[...], kept[rows, cols], NN).astype(BF16)
            block = (pl.ds(at * quarter, quarter), pl.ds(start, size))
            sent.append(pltpu.make_async_copy(moved.at[block], out_ref.at[block], out_sems.at[len(sent)]))
            sent[-1].start()
    for copy in sent:
        copy.wait()


def keep(meta, select, p_table, h_table):
    shape = (2 * p_table.shape[1], KEPT * TILE)
    return call(
        keep_kernel,
        "keep",
        out_shape=pltpu.HBM(shape, BF16),
        in_specs=[IN_SMEM, IN_VMEM] + [IN_PLACE] * 2,
        out_specs=IN_PLACE,
        scratch_shapes=[
            pltpu.VMEM(shape, BF16),
            pltpu.VMEM(shape, BF16),
            pltpu.SemaphoreType.DMA((2 * (2 + SHARED),)),
            pltpu.SemaphoreType.DMA((2 * N_BLOCKS,)),
        ],
    )(meta, select, *in_hbm(p_table, h_table))


def last_rows(slot, owners):
    i = lax.broadcasted_iota(jnp.int32, (4 * owners, 1), 0)
    hit = ((i >> 2) << 3) + (i & 3) + 4 * slot == lax.broadcasted_iota(jnp.int32, (4 * owners, 8 * owners), 1)
    return jnp.where(hit, 1.0, 0.0).astype(BF16)


def forward_kernel(part, meta, rate, mask, weight, recv, table, factor, keep, send, *refs):
    del factor
    owners, both, width = recv.shape
    source, (table, wind, spec, sems) = table, refs
    copies = []
    for n in range(N_BLOCKS):
        cols = pl.ds(n * STREAM, min(STREAM, KEPT * TILE - n * STREAM))
        copies.append(pltpu.make_async_copy(source.at[:, cols], table.at[:, cols], sems.at[n]))
        copies[n].start()
    waited = 0
    quarter = weight.shape[0]
    levels = width // 4
    main = owners * 16
    columns = [slice(at * levels, (at + 1) * levels) for at in (part, 3 - part)]
    mixed = [recv[:, 32:, cols].astype(F32).reshape(owners * 8, levels).astype(BF16) for cols in columns]
    mixed = jnp.concatenate(mixed, axis=1)
    for slot in range(2):
        rows = [recv[:, 16 * slot:16 * slot + 16, cols].reshape(main, levels).astype(F32) for cols in columns]
        rows = [jnp.concatenate(rows, axis=1), dot(last_rows(slot, owners), mixed, NN)]
        weighted = jnp.concatenate(rows, axis=0) * weight[...]
        wind[slot] = weighted.T.astype(BF16)
    split = (SURE[0] + SHARED) * TILE
    for slot in range(2):
        low, high = (0, split) if slot == 0 else (SURE[0] * TILE, KEPT * TILE)
        r = rate[slot]
        w = wind[slot]
        for start in range(low, high, BLOCK):
            cols = slice(start, min(start + BLOCK, high))
            while waited < len(copies) and waited * STREAM < cols.stop:
                copies[waited].wait()
                waited += 1
            proj_p = dot(w, table[:quarter, cols], NN)
            proj_h = dot(w, table[quarter:, cols], NN)
            psi = proj_h[:levels] - r * proj_p[levels:]
            chi = r * proj_p[:levels] - proj_h[levels:]
            if slot == 1 and start < split:
                first = mask[:, cols] > 0.5
                psi = jnp.where(first, spec[:levels, cols], psi)
                chi = jnp.where(first, spec[levels:, cols], chi)
            spec[:levels, cols] = psi
            spec[levels:, cols] = chi
    lane = lax.broadcasted_iota(jnp.int32, (2 * levels, TILE), 1)
    at = pl.ds(pl.multiple_of(meta[AT] * TILE, TILE), TILE)
    last, other = spec[:, CUT:CUT + TILE], spec[:, at]
    all_first = meta[ALL_FIRST] == 1
    low_first, low_second = jnp.where(all_first, last, other), jnp.where(all_first, other, last)
    spec[:, at] = jnp.where(lane >= meta[LANE], low_first, pltpu.roll(low_second, meta[LANE], 1))
    mine = pl.multiple_of(meta[HALF] * levels, levels)
    for ref, start in ((keep, mine), (send, levels - mine)):
        rows = pl.ds(pl.multiple_of(start, levels), levels)
        ref[:, :CUT] = spec[rows, :CUT].astype(ref.dtype)
        ref[:, CUT:] = spec[rows, CUT + TILE:].astype(ref.dtype)


def forward(part, meta, rate, mask, weight, recv, table, factor):
    owners, both, width = recv.shape
    levels = width // 4
    quarter = weight.shape[0]
    out_shape = [jax.ShapeDtypeStruct((levels, SENT), F32), jax.ShapeDtypeStruct((levels, SENT), BF16)]
    scratch = [
        pltpu.VMEM((2, 2 * levels, quarter), BF16),
        pltpu.VMEM((2 * levels, KEPT * TILE), F32),
        pltpu.SemaphoreType.DMA((N_BLOCKS,)),
    ]
    (scratch, out_shape)[part].insert((0, 2)[part], pltpu.VMEM(table.shape, BF16))
    return call(
        functools.partial(forward_kernel, part),
        "forward",
        in_specs=[IN_SMEM] * 2 + [IN_VMEM] * 3 + [IN_PLACE] * 2,
        out_specs=[IN_VMEM] * len(out_shape),
        out_shape=out_shape,
        scratch_shapes=scratch,
        cost_estimate=pl.CostEstimate(flops=5 * 10**9, bytes_accessed=10**7, transcendentals=0),
    )(meta, rate, mask, weight, recv, *in_hbm(table), factor)


def backward_kernel(meta, halves, rate, mask, first_part, second_part, table, *refs):
    out_ref, every, masked, last, out, sems = refs[-6:]
    levels = first_part.shape[0]
    quarter = table.shape[0] // 2
    owners = out.shape[1]
    main = owners * 16
    split = (SURE[0] + SHARED) * TILE
    degrees = KEPT * TILE
    every[:levels] = first_part[...]
    every[levels:] = second_part[...]
    shared = slice(SURE[0] * TILE, split)
    cut = CUT - shared.start
    first = mask[:, shared.start:CUT] > 0.5
    both_slots = every[:, shared.start:CUT].astype(F32)
    lane = lax.broadcasted_iota(jnp.int32, (2 * levels, TILE), 1)
    joint = every[:, pl.ds(pl.multiple_of(meta[AT_SENT] * TILE, TILE), TILE)].astype(F32)
    back = TILE - meta[LANE]
    low_first = jnp.where(lane >= meta[LANE], joint, 0.0).astype(BF16)
    low_second = jnp.where(lane >= back, pltpu.roll(joint, back & (TILE - 1), 1), 0.0).astype(BF16)
    masked[0, :, :shared.start] = every[:, :shared.start]
    masked[0, :, shared.start:CUT] = jnp.where(first, both_slots, 0.0).astype(BF16)
    masked[1, :, :cut] = jnp.where(first, 0.0, both_slots).astype(BF16)
    masked[1, :, cut + TILE:degrees - shared.start] = every[:, CUT:]

    @pl.when(meta[ALL_FIRST] == 1)
    def _():
        masked[0, :, CUT:split] = low_first
        masked[1, :, cut:cut + TILE] = jnp.zeros_like(low_second)
        masked[1, :, cut + TILE:cut + 2 * TILE] = low_second

    @pl.when(meta[ALL_FIRST] != 1)
    def _():
        masked[0, :, CUT:split] = jnp.zeros_like(low_first)
        masked[0, :, pl.ds(pl.multiple_of(meta[AT] * TILE, TILE), TILE)] = low_first
        masked[1, :, cut:cut + TILE] = low_second

    for slot in range(2):
        low, high = (0, split) if slot == 0 else (shared.start, degrees)
        pot = masked[slot, :, :high - low]
        sum_p, sum_h = [dot(table[n * quarter:(n + 1) * quarter, low:high], pot, NT) for n in range(2)]
        for part in range(2):
            cols = slice(part * levels, (part + 1) * levels)
            r = rate[slot] if part == 0 else -rate[slot]
            p, h = r * sum_p[:, cols], sum_h[:, cols]
            of_psi = halves[part] == 0
            for n, field in enumerate((jnp.where(of_psi, -h, -p), jnp.where(of_psi, p, h))):
                field = field.astype(BF16)
                out[2 * part + n, :, 16 * slot:16 * slot + 16] = field[:main].reshape(owners, 16, levels)
                last[slot, :, (2 * part + n) * levels:(2 * part + n + 1) * levels] = field[main:]
    mixed = dot(last_rows(0, owners), last[0], TN) + dot(last_rows(1, owners), last[1], TN)
    sent = []
    for n in range(4):
        some = mixed[:, n * levels:(n + 1) * levels]
        out[n, :, 32:] = some.reshape(owners, 8, levels).astype(BF16)
        column = pl.multiple_of((2 * n + halves[n // 2]) * levels, levels)
        sent.append(pltpu.make_async_copy(out.at[n], out_ref.at[:, :, pl.ds(column, levels)], sems.at[n]))
        sent[n].start()
    for copy in sent:
        copy.wait()


def backward(meta, halves, rate, mask, first_part, second_part, table, payload, filled=()):
    levels = first_part.shape[0]
    owners, both, width = payload
    return call(
        backward_kernel,
        "backward",
        in_specs=[IN_SMEM] * 3 + [IN_VMEM] * 4 + [IN_PLACE] * len(filled),
        out_specs=IN_PLACE,
        out_shape=pltpu.HBM(payload, BF16),
        input_output_aliases={7: 0} if filled else {},
        scratch_shapes=[
            pltpu.VMEM((2 * levels, SENT), BF16),
            pltpu.VMEM((2, 2 * levels, (SURE[0] + SHARED) * TILE), BF16),
            pltpu.VMEM((2, owners * 4, 4 * levels), BF16),
            pltpu.VMEM((4, owners, both, levels), BF16),
            pltpu.SemaphoreType.DMA((4,)),
        ],
    )(meta, halves, rate, mask, first_part, second_part, table, *filled)


def add_kernel(kept, got, total, sent):
    total[...] = kept[...] + got[...].astype(F32)
    sent[...] = total[...].astype(BF16)


def add(kept, got):
    return call(
        add_kernel,
        "add",
        in_specs=[IN_VMEM] * 2,
        out_specs=[IN_VMEM] * 2,
        out_shape=[jax.ShapeDtypeStruct(kept.shape, F32), jax.ShapeDtypeStruct(kept.shape, BF16)],
    )(kept, got)


def scale_kernel(kept, got, factor, mine):
    mine[...] = ((kept[...] + got[...].astype(F32)) * factor[...]).astype(BF16)


def scale(kept, got, factor):
    return call(
        scale_kernel,
        "scale",
        in_specs=[IN_VMEM] * 3,
        out_specs=IN_VMEM,
        out_shape=jax.ShapeDtypeStruct(kept.shape, BF16),
    )(kept, got, factor)


def layout(wavenumbers, count, half):
    low_first, low_second = wavenumbers[0] // TILE, wavenumbers[1] // TILE
    n_first = count - low_first - SURE[0]
    k = jnp.arange(SHARED)
    shared_slot = (k >= n_first).astype(jnp.int32)
    shared_tile = jnp.where(k < n_first, count - SURE[0] - 1 - k, count - SURE[1] - 1 - (k - n_first))
    slot = jnp.concatenate([jnp.zeros(SURE[0], jnp.int32), shared_slot, jnp.ones(SURE[1], jnp.int32)])
    mask = jnp.repeat(1.0 - slot.astype(F32), TILE)[None, :]
    all_first = n_first == SHARED
    at = jnp.where(n_first == 0, 0, SURE[0] - 1 + n_first)
    at, at_sent = jnp.where(all_first, SURE[0] + SHARED, at), jnp.where(all_first, SURE[0] + SHARED - 1, at)
    lane_first = wavenumbers[0] % TILE
    scalars = jnp.stack([half, all_first.astype(jnp.int32), lane_first, at, at_sent])
    meta = jnp.concatenate([shared_slot, shared_tile, scalars]).astype(jnp.int32)
    tile = jnp.concatenate([jnp.arange(count - SURE[0], count), shared_tile[:-1], jnp.arange(count - SURE[1], count)])
    joint = jnp.arange(tile.shape[0]) == at_sent
    lane = jnp.arange(TILE)
    degree = jnp.where(joint, low_first, tile)[:, None] * TILE + lane[None, :]
    degree_second = low_second * TILE + TILE + lane - lane_first
    degree = jnp.where(joint[:, None] & (lane < lane_first)[None, :], degree_second[None, :], degree).astype(F32)
    factor = (-(LMAX * LMAX * 1.0) / jnp.maximum(degree * (degree + 1.0), 1.0)).reshape(1, -1)
    return meta, mask, factor


def on_device(fourier_wind, quad_weight, p_table, h_table, wavenumbers, row_latitude):
    owners = lax.axis_size("ma")
    groups = lax.axis_size("oct")
    me = lax.axis_index("oct")
    rows = fourier_wind.shape[0]
    quarter = p_table.shape[1]
    count = p_table.shape[2] // TILE
    flip, turn = [z ^ 1 for z in range(groups)], [groups - 1 - z for z in range(groups)]
    ways = [
        [(d * groups + z, d * groups + (flip, turn)[(d + n) % 2][z]) for d in range(owners) for z in range(groups)]
        for n in range(2)]
    halves = ((me + 1) // 2) % 2, me // 2
    odd = lax.axis_index("ma") % 2

    def swap(x, pairs):
        return lax.ppermute(x, ("ma", "oct"), pairs)

    received = lax.all_to_all(pack(fourier_wind), "ma", 0, 0, tiled=True)

    metas = []
    for n in range(2):
        half = jnp.where(odd == n, *halves)
        meta, mask, factor = layout(wavenumbers, count, half)
        metas.append(meta)
    rate = wavenumbers.astype(F32) / LMAX

    local = lax.dynamic_index_in_dim(row_latitude.reshape(owners, groups, rows), me, 1, keepdims=False) - me * quarter
    target = jnp.concatenate([local[:, :16].reshape(-1), local[:, 16:].reshape(-1)])[:, None]
    hit = target == jnp.arange(quarter)[None, :]
    weight = jnp.sum(jnp.where(hit, quad_weight[None, :], 0.0), axis=1, keepdims=True)
    table = keep(meta, hit.astype(BF16), p_table, h_table)
    owners, both, width = received.shape
    payload = (owners, both, 2 * width)
    signs = (rate, -rate)
    kept_a, sent_a = forward(0, metas[0], signs[0], mask, weight, received, table, factor)
    kept_b, sent_b, table = forward(1, metas[1], signs[1], mask, weight, received, table, factor)
    table = pltpu.with_memory_space_constraint(table, pltpu.VMEM)
    kept_a, sent_a = add(kept_a, swap(sent_a, ways[0]))
    kept_b, sent_b = add(kept_b, swap(sent_b, ways[1]))
    mine_a = scale(kept_a, swap(sent_a, ways[1]), factor)
    mine_b = scale(kept_b, swap(sent_b, ways[0]), factor)
    theirs_a, theirs_b = swap(mine_a, ways[0]), swap(mine_b, ways[1])
    halves = jnp.stack([meta[HALF] for meta in metas])
    out = backward(metas[0], halves, rate, mask, mine_a, mine_b, table, payload)
    out = backward(metas[0], 1 - halves, rate, mask, theirs_a, theirs_b, table, payload, (out,))
    return tuple(unpack(lax.all_to_all(out, "ma", 0, 0, tiled=True), rows))


def solution(mesh):
    placed = (
        P(("ma", "oct"), None, None),
        P("oct"),
        P("ma", "oct", None),
        P("ma", "oct", None),
        P("ma"),
        P(),
    )
    return jax.shard_map(
        on_device,
        mesh=mesh,
        in_specs=placed,
        out_specs=(P(("ma", "oct"), None, None), P(("ma", "oct"), None, None)),
        check_vma=False,
    )
```

```python
import jax
import jax.numpy as jnp
from jax import lax
from jax.experimental import pallas as pl
from jax.experimental.pallas import tpu as pltpu
from jax.sharding import PartitionSpec as P

LMAX = 2559
TILE = 128
SURE = (11, 5)
SHARED = 5
KEPT = SURE[0] + SHARED + SURE[1]
CUT = (SURE[0] + SHARED - 1) * TILE
SENT = (KEPT - 1) * TILE
HALF, ALL_FIRST, LANE, AT, AT_SENT, PART = range(2 * SHARED, 2 * SHARED + 6)
BLOCK = 512
STREAM = 512
N_BLOCKS = -(-KEPT * TILE // STREAM)
BF16 = jnp.bfloat16
F32 = jnp.float32
LIMIT = 32 * 1024 * 1024
IN_VMEM = pl.BlockSpec(memory_space=pltpu.VMEM)
IN_SMEM = pl.BlockSpec(memory_space=pltpu.SMEM)
IN_PLACE = pl.BlockSpec(memory_space=pl.ANY)
NN = ((1,), (0,))
TN = ((0,), (0,))
NT = ((1,), (1,))


def dot(a, b, dims):
    return lax.dot_general(a, b, (dims, ((), ())), preferred_element_type=F32)


def call(kernel, name, **kwargs):
    return pl.pallas_call(
        kernel, name=name, compiler_params=pltpu.CompilerParams(vmem_limit_bytes=LIMIT), **kwargs)


def fill_order(order, source):
    size = order.shape[0]
    index = source(lax.broadcasted_iota(jnp.int32, (size, 1), 0))
    hit = index == lax.broadcasted_iota(jnp.int32, (size, size), 1)
    order[...] = jnp.where(hit, 1.0, 0.0).astype(BF16)


def log2(n):
    return n.bit_length() - 1


def pack_kernel(wind_ref, out_ref, order8, order4):
    rows, slots, lanes = wind_ref.shape

    @pl.when(pl.program_id(0) == 0)
    def _():
        for count, order in ((8, order8), (4, order4)):
            c = log2(count)
            fill_order(order, lambda i: (i & (count - 1)) * slots + ((i >> (c + 1)) << 1) + ((i >> c) & 1))

    eights = []
    for start in (0, 8, 16):
        count, order = (8, order8) if start < 16 else (4, order4)
        block = wind_ref[start:start + count].reshape(count * slots, lanes)
        eights.append(dot(order[...], block, NN).reshape(slots // 2, 2 * count, lanes))
    for slot in range(2):
        rows_of = [x[:, 8 * slot:8 * slot + 8] for x in eights[:2]]
        out_ref[:, 16 * slot:16 * slot + 16] = jnp.concatenate(rows_of, axis=1).astype(BF16)
    out_ref[:, 32:] = eights[2].astype(BF16)


def pack(wind):
    rows, slots, width = wind.shape
    lanes = width // 2
    return call(
        pack_kernel,
        "pack",
        grid=(2,),
        out_shape=pltpu.HBM((slots // 2, rows * 2, width), BF16),
        in_specs=[pl.BlockSpec((rows, slots, lanes), lambda i: (0, 0, i))],
        out_specs=pl.BlockSpec((slots // 2, rows * 2, lanes), lambda i: (0, 0, i)),
        scratch_shapes=[
            pltpu.VMEM((8 * slots, 8 * slots), BF16),
            pltpu.VMEM((4 * slots, 4 * slots), BF16),
        ],
    )(*in_hbm(wind))


def unpack_kernel(halves, payload, *refs):
    rot_ref, div_ref, outs, order8, order4, sems = refs[-6:]
    _, rows, slots, lanes = outs.shape
    for count, order in ((8, order8), (4, order4)):
        c = log2(count)

        def source(i):
            slot = i & (slots - 1)
            return ((slot >> 1) << (c + 1)) + ((slot & 1) << c) + (i >> log2(slots))

        fill_order(order, source)
    copies = []
    for part in range(2):
        cols = slice(2 * part * lanes, 2 * (part + 1) * lanes)
        mains = [payload[:, 16 * slot:16 * slot + 16, cols].astype(F32) for slot in range(2)]
        for start in (0, 8, 16):
            if start < 16:
                block = jnp.concatenate([x[:, start:start + 8] for x in mains], axis=1)
                count, order = 8, order8
            else:
                block = payload[:, 32:, cols].astype(F32)
                count, order = 4, order4
            moved = dot(order[...], block.reshape(count * slots, 2 * lanes).astype(BF16), NN)
            moved = moved.reshape(count, slots, 2 * lanes).astype(BF16)
            for k in range(2):
                outs[2 * part + k, start:start + count] = moved[:, :, k * lanes:(k + 1) * lanes]
        for k, component in enumerate((part, 3 - part)):
            n = 2 * part + k
            at = (slice(None), slice(None), pl.ds(component * lanes, lanes))
            copies.append([pltpu.make_async_copy(outs.at[n], ref.at[at], sems.at[n]) for ref in (rot_ref, div_ref)])
            for half in range(2):
                pl.when(halves[part] == half)(copies[n][half].start)
    for to_rot, _ in copies:
        to_rot.wait()


def unpack(halves, payload, rows, filled=()):
    pairs, both, width = payload.shape
    slots = pairs * 2
    shape = (rows, slots, width)
    return call(
        unpack_kernel,
        "unpack",
        out_shape=(pltpu.HBM(shape, BF16), pltpu.HBM(shape, BF16)),
        in_specs=[IN_SMEM, IN_VMEM] + [IN_PLACE] * len(filled),
        out_specs=(IN_PLACE, IN_PLACE),
        input_output_aliases={2: 0, 3: 1} if filled else {},
        scratch_shapes=[
            pltpu.VMEM((4, rows, slots, width // 4), BF16),
            pltpu.VMEM((8 * slots, 8 * slots), BF16),
            pltpu.VMEM((4 * slots, 4 * slots), BF16),
            pltpu.SemaphoreType.DMA((4,)),
        ],
    )(halves, payload, *filled)


def in_hbm(*arrays):
    return [pltpu.with_memory_space_constraint(x, pltpu.HBM) for x in arrays]


def keep_kernel(meta, select, p_ref, h_ref, out_ref, kept, moved, sems, out_sems):
    quarter, degrees = p_ref.shape[1:]
    pieces = [(0, degrees - SURE[0] * TILE, SURE[0], 0)]
    for k in range(SHARED):
        pieces.append((meta[k], pl.multiple_of(meta[SHARED + k] * TILE, TILE), 1, SURE[0] + k))
    pieces.append((1, degrees - SURE[1] * TILE, SURE[1], SURE[0] + SHARED))
    copies = []
    for at, ref in enumerate((p_ref, h_ref)):
        for slot, source, count, target in pieces:
            copies.append(pltpu.make_async_copy(
                ref.at[slot, :, pl.ds(source, count * TILE)],
                kept.at[pl.ds(at * quarter, quarter), pl.ds(target * TILE, count * TILE)],
                sems.at[len(copies)],
            ))
            copies[-1].start()
    sent = []
    for at in range(2):
        for copy in copies[at * len(pieces):(at + 1) * len(pieces)]:
            copy.wait()
        rows = slice(at * quarter, (at + 1) * quarter)
        for n in range(N_BLOCKS):
            start, size = n * STREAM, min(STREAM, KEPT * TILE - n * STREAM)
            cols = slice(start, start + size)
            moved[rows, cols] = dot(select[...], kept[rows, cols], NN).astype(BF16)
            block = (pl.ds(at * quarter, quarter), pl.ds(start, size))
            sent.append(pltpu.make_async_copy(moved.at[block], out_ref.at[block], out_sems.at[len(sent)]))
            sent[-1].start()
    for copy in sent:
        copy.wait()


def keep(meta, select, p_table, h_table):
    shape = (2 * p_table.shape[1], KEPT * TILE)
    return call(
        keep_kernel,
        "keep",
        out_shape=pltpu.HBM(shape, BF16),
        in_specs=[IN_SMEM, IN_VMEM] + [IN_PLACE] * 2,
        out_specs=IN_PLACE,
        scratch_shapes=[
            pltpu.VMEM(shape, BF16),
            pltpu.VMEM(shape, BF16),
            pltpu.SemaphoreType.DMA((2 * (2 + SHARED),)),
            pltpu.SemaphoreType.DMA((2 * N_BLOCKS,)),
        ],
    )(meta, select, *in_hbm(p_table, h_table))


def last_rows(slot, owners):
    i = lax.broadcasted_iota(jnp.int32, (4 * owners, 1), 0)
    hit = ((i >> 2) << 3) + (i & 3) + 4 * slot == lax.broadcasted_iota(jnp.int32, (4 * owners, 8 * owners), 1)
    return jnp.where(hit, 1.0, 0.0).astype(BF16)


def forward_kernel(meta, rate, mask, weight, recv, table, factor, keep, send, *refs):
    del factor
    owners, both, width = recv.shape
    source, (table, wind, spec, sems) = table, refs
    copies = []
    for n in range(N_BLOCKS):
        cols = pl.ds(n * STREAM, min(STREAM, KEPT * TILE - n * STREAM))
        copies.append(pltpu.make_async_copy(source.at[:, cols], table.at[:, cols], sems.at[n]))
        copies[n].start()
    waited = 0
    quarter = weight.shape[0]
    levels = width // 4
    main = owners * 16
    columns = [pl.ds(pl.multiple_of(at * levels, levels), levels) for at in (meta[PART], 3 - meta[PART])]
    mixed = [recv[:, 32:, cols].astype(F32).reshape(owners * 8, levels).astype(BF16) for cols in columns]
    mixed = jnp.concatenate(mixed, axis=1)
    for slot in range(2):
        rows = [recv[:, 16 * slot:16 * slot + 16, cols].reshape(main, levels).astype(F32) for cols in columns]
        rows = [jnp.concatenate(rows, axis=1), dot(last_rows(slot, owners), mixed, NN)]
        weighted = jnp.concatenate(rows, axis=0) * weight[...]
        wind[slot] = weighted.T.astype(BF16)
    split = (SURE[0] + SHARED) * TILE
    for slot in range(2):
        low, high = (0, split) if slot == 0 else (SURE[0] * TILE, KEPT * TILE)
        r = rate[slot]
        w = wind[slot]
        for start in range(low, high, BLOCK):
            cols = slice(start, min(start + BLOCK, high))
            while waited < len(copies) and waited * STREAM < cols.stop:
                copies[waited].wait()
                waited += 1
            proj_p = dot(w, table[:quarter, cols], NN)
            proj_h = dot(w, table[quarter:, cols], NN)
            psi = proj_h[:levels] - r * proj_p[levels:]
            chi = r * proj_p[:levels] - proj_h[levels:]
            if slot == 1 and start < split:
                first = mask[:, cols] > 0.5
                psi = jnp.where(first, spec[:levels, cols], psi)
                chi = jnp.where(first, spec[levels:, cols], chi)
            spec[:levels, cols] = psi
            spec[levels:, cols] = chi
    lane = lax.broadcasted_iota(jnp.int32, (2 * levels, TILE), 1)
    at = pl.ds(pl.multiple_of(meta[AT] * TILE, TILE), TILE)
    last, other = spec[:, CUT:CUT + TILE], spec[:, at]
    all_first = meta[ALL_FIRST] == 1
    low_first, low_second = jnp.where(all_first, last, other), jnp.where(all_first, other, last)
    spec[:, at] = jnp.where(lane >= meta[LANE], low_first, pltpu.roll(low_second, meta[LANE], 1))
    mine = pl.multiple_of(meta[HALF] * levels, levels)
    for ref, start in ((keep, mine), (send, levels - mine)):
        rows = pl.ds(pl.multiple_of(start, levels), levels)
        ref[:, :CUT] = spec[rows, :CUT].astype(ref.dtype)
        ref[:, CUT:] = spec[rows, CUT + TILE:].astype(ref.dtype)


def forward(last, meta, rate, mask, weight, recv, table, factor):
    owners, both, width = recv.shape
    levels = width // 4
    quarter = weight.shape[0]
    out_shape = [jax.ShapeDtypeStruct((levels, SENT), F32), jax.ShapeDtypeStruct((levels, SENT), BF16)]
    scratch = [
        pltpu.VMEM((2, 2 * levels, quarter), BF16),
        pltpu.VMEM((2 * levels, KEPT * TILE), F32),
        pltpu.SemaphoreType.DMA((N_BLOCKS,)),
    ]
    (scratch, out_shape)[last].insert((0, 2)[last], pltpu.VMEM(table.shape, BF16))
    return call(
        forward_kernel,
        "forward",
        in_specs=[IN_SMEM] * 2 + [IN_VMEM] * 3 + [IN_PLACE] * 2,
        out_specs=[IN_VMEM] * len(out_shape),
        out_shape=out_shape,
        scratch_shapes=scratch,
        cost_estimate=pl.CostEstimate(flops=5 * 10**9, bytes_accessed=10**7, transcendentals=0),
    )(meta, rate, mask, weight, recv, *in_hbm(table), factor)


def backward_kernel(meta, halves, rate, mask, first_part, second_part, table, out_ref, every, masked, last, out, sems):
    levels = first_part.shape[0]
    quarter = table.shape[0] // 2
    owners = out.shape[0]
    main = owners * 16
    split = (SURE[0] + SHARED) * TILE
    degrees = KEPT * TILE
    every[:levels] = first_part[...]
    every[levels:] = second_part[...]
    shared = slice(SURE[0] * TILE, split)
    cut = CUT - shared.start
    first = mask[:, shared.start:CUT] > 0.5
    both_slots = every[:, shared.start:CUT].astype(F32)
    lane = lax.broadcasted_iota(jnp.int32, (2 * levels, TILE), 1)
    joint = every[:, pl.ds(pl.multiple_of(meta[AT_SENT] * TILE, TILE), TILE)].astype(F32)
    back = TILE - meta[LANE]
    low_first = jnp.where(lane >= meta[LANE], joint, 0.0).astype(BF16)
    low_second = jnp.where(lane >= back, pltpu.roll(joint, back & (TILE - 1), 1), 0.0).astype(BF16)
    masked[0, :, :shared.start] = every[:, :shared.start]
    masked[0, :, shared.start:CUT] = jnp.where(first, both_slots, 0.0).astype(BF16)
    masked[1, :, :cut] = jnp.where(first, 0.0, both_slots).astype(BF16)
    masked[1, :, cut + TILE:degrees - shared.start] = every[:, CUT:]

    @pl.when(meta[ALL_FIRST] == 1)
    def _():
        masked[0, :, CUT:split] = low_first
        masked[1, :, cut:cut + TILE] = jnp.zeros_like(low_second)
        masked[1, :, cut + TILE:cut + 2 * TILE] = low_second

    @pl.when(meta[ALL_FIRST] != 1)
    def _():
        masked[0, :, CUT:split] = jnp.zeros_like(low_first)
        masked[0, :, pl.ds(pl.multiple_of(meta[AT] * TILE, TILE), TILE)] = low_first
        masked[1, :, cut:cut + TILE] = low_second

    for slot in range(2):
        low, high = (0, split) if slot == 0 else (shared.start, degrees)
        pot = masked[slot, :, :high - low]
        sum_p, sum_h = [dot(table[n * quarter:(n + 1) * quarter, low:high], pot, NT) for n in range(2)]
        for part in range(2):
            cols = slice(part * levels, (part + 1) * levels)
            r = rate[slot] if part == 0 else -rate[slot]
            p, h = r * sum_p[:, cols], sum_h[:, cols]
            of_psi = halves[part] == 0
            for n, field in enumerate((jnp.where(of_psi, -h, -p), jnp.where(of_psi, p, h))):
                field = field.astype(BF16)
                at = slice((2 * part + n) * levels, (2 * part + n + 1) * levels)
                out[:, 16 * slot:16 * slot + 16, at] = field[:main].reshape(owners, 16, levels)
                last[slot, :, at] = field[main:]
    mixed = dot(last_rows(0, owners), last[0], TN) + dot(last_rows(1, owners), last[1], TN)
    out[:, 32:] = mixed.reshape(owners, 8, 4 * levels).astype(BF16)
    sent = []
    for n, part in enumerate((meta[PART], 1 - meta[PART])):
        column = pl.multiple_of(part * 2 * levels, 2 * levels)
        sent.append(pltpu.make_async_copy(
            out.at[:, :, pl.ds(n * 2 * levels, 2 * levels)], out_ref.at[:, :, pl.ds(column, 2 * levels)], sems.at[n]))
        sent[n].start()
    for copy in sent:
        copy.wait()


def backward(meta, halves, rate, mask, first_part, second_part, table, payload, flops):
    levels = first_part.shape[0]
    owners, both, width = payload
    return call(
        backward_kernel,
        "backward",
        in_specs=[IN_SMEM] * 3 + [IN_VMEM] * 4,
        out_specs=IN_PLACE,
        out_shape=pltpu.HBM(payload, BF16),
        scratch_shapes=[
            pltpu.VMEM((2 * levels, SENT), BF16),
            pltpu.VMEM((2, 2 * levels, (SURE[0] + SHARED) * TILE), BF16),
            pltpu.VMEM((2, owners * 4, 4 * levels), BF16),
            pltpu.VMEM(payload, BF16),
            pltpu.SemaphoreType.DMA((2,)),
        ],
        cost_estimate=pl.CostEstimate(flops=flops, bytes_accessed=10**7, transcendentals=0),
    )(meta, halves, rate, mask, first_part, second_part, table)


def add_kernel(kept, got, total, sent):
    total[...] = kept[...] + got[...].astype(F32)
    sent[...] = total[...].astype(BF16)


def add(kept, got):
    return call(
        add_kernel,
        "add",
        in_specs=[IN_VMEM] * 2,
        out_specs=[IN_VMEM] * 2,
        out_shape=[jax.ShapeDtypeStruct(kept.shape, F32), jax.ShapeDtypeStruct(kept.shape, BF16)],
    )(kept, got)


def scale_kernel(kept, got, factor, mine):
    mine[...] = ((kept[...] + got[...].astype(F32)) * factor[...]).astype(BF16)


def scale(kept, got, factor):
    return call(
        scale_kernel,
        "scale",
        in_specs=[IN_VMEM] * 3,
        out_specs=IN_VMEM,
        out_shape=jax.ShapeDtypeStruct(kept.shape, BF16),
    )(kept, got, factor)


def layout(wavenumbers, count, half, part):
    low_first, low_second = wavenumbers[0] // TILE, wavenumbers[1] // TILE
    n_first = count - low_first - SURE[0]
    k = jnp.arange(SHARED)
    shared_slot = (k >= n_first).astype(jnp.int32)
    shared_tile = jnp.where(k < n_first, count - SURE[0] - 1 - k, count - SURE[1] - 1 - (k - n_first))
    slot = jnp.concatenate([jnp.zeros(SURE[0], jnp.int32), shared_slot, jnp.ones(SURE[1], jnp.int32)])
    mask = jnp.repeat(1.0 - slot.astype(F32), TILE)[None, :]
    all_first = n_first == SHARED
    at = jnp.where(n_first == 0, 0, SURE[0] - 1 + n_first)
    at, at_sent = jnp.where(all_first, SURE[0] + SHARED, at), jnp.where(all_first, SURE[0] + SHARED - 1, at)
    lane_first = wavenumbers[0] % TILE
    scalars = jnp.stack([half, all_first.astype(jnp.int32), lane_first, at, at_sent, part])
    meta = jnp.concatenate([shared_slot, shared_tile, scalars]).astype(jnp.int32)
    tile = jnp.concatenate([jnp.arange(count - SURE[0], count), shared_tile[:-1], jnp.arange(count - SURE[1], count)])
    joint = jnp.arange(tile.shape[0]) == at_sent
    lane = jnp.arange(TILE)
    degree = jnp.where(joint, low_first, tile)[:, None] * TILE + lane[None, :]
    degree_second = low_second * TILE + TILE + lane - lane_first
    degree = jnp.where(joint[:, None] & (lane < lane_first)[None, :], degree_second[None, :], degree).astype(F32)
    factor = (-(LMAX * LMAX * 1.0) / jnp.maximum(degree * (degree + 1.0), 1.0)).reshape(1, -1)
    return meta, mask, factor


def on_device(fourier_wind, quad_weight, p_table, h_table, wavenumbers, row_latitude):
    owners = lax.axis_size("ma")
    groups = lax.axis_size("oct")
    me = lax.axis_index("oct")
    rows = fourier_wind.shape[0]
    quarter = p_table.shape[1]
    count = p_table.shape[2] // TILE
    flip, turn = [z ^ 1 for z in range(groups)], [groups - 1 - z for z in range(groups)]
    ways = [
        [(d * groups + z, d * groups + (flip, turn)[(d + n) % 2][z]) for d in range(owners) for z in range(groups)]
        for n in range(2)]
    halves = ((me + 1) // 2) % 2, me // 2
    odd = lax.axis_index("ma") % 2

    def swap(x, pairs):
        return lax.ppermute(x, ("ma", "oct"), pairs)

    received = lax.all_to_all(pack(fourier_wind), "ma", 0, 0, tiled=True)

    metas = []
    for n in range(2):
        half = jnp.where(odd == n, *halves)
        meta, mask, factor = layout(wavenumbers, count, half, odd ^ n)
        metas.append(meta)
    rate = wavenumbers.astype(F32) / LMAX

    local = lax.dynamic_index_in_dim(row_latitude.reshape(owners, groups, rows), me, 1, keepdims=False) - me * quarter
    target = jnp.concatenate([local[:, :16].reshape(-1), local[:, 16:].reshape(-1)])[:, None]
    hit = target == jnp.arange(quarter)[None, :]
    weight = jnp.sum(jnp.where(hit, quad_weight[None, :], 0.0), axis=1, keepdims=True)
    table = keep(meta, hit.astype(BF16), p_table, h_table)
    owners, both, width = received.shape
    rate = jnp.where(odd == 0, rate, -rate)
    signs = (rate, -rate)
    kept_a, sent_a = forward(0, metas[0], signs[0], mask, weight, received, table, factor)
    kept_b, sent_b, table = forward(1, metas[1], signs[1], mask, weight, received, table, factor)
    table = pltpu.with_memory_space_constraint(table, pltpu.VMEM)
    kept_a, sent_a = add(kept_a, swap(sent_a, ways[0]))
    kept_b, sent_b = add(kept_b, swap(sent_b, ways[1]))
    mine_a = scale(kept_a, swap(sent_a, ways[1]), factor)
    mine_b = scale(kept_b, swap(sent_b, ways[0]), factor)
    theirs_a, theirs_b = swap(mine_a, ways[0]), swap(mine_b, ways[1])
    kept_halves = jnp.stack([meta[HALF] for meta in metas])
    kept = backward(metas[0], kept_halves, rate, mask, mine_a, mine_b, table, received.shape, 50000000000)
    others = backward(metas[0], 1 - kept_halves, rate, mask, theirs_a, theirs_b, table, received.shape, 600000000000)
    kept, others = (lax.all_to_all(x, "ma", 0, 0, tiled=True) for x in (kept, others))
    halves = jnp.stack(halves).astype(jnp.int32)
    return tuple(unpack(1 - halves, others, rows, unpack(halves, kept, rows)))


def solution(mesh):
    placed = (
        P(("ma", "oct"), None, None),
        P("oct"),
        P("ma", "oct", None),
        P("ma", "oct", None),
        P("ma"),
        P(),
    )
    return jax.shard_map(
        on_device,
        mesh=mesh,
        in_specs=placed,
        out_specs=(P(("ma", "oct"), None, None), P(("ma", "oct"), None, None)),
        check_vma=False,
    )
```

```python
import jax
import jax.numpy as jnp
from jax import lax
from jax.experimental import pallas as pl
from jax.experimental.pallas import tpu as pltpu
from jax.sharding import PartitionSpec as P

LMAX = 2559
TILE = 128
SURE = (11, 5)
SHARED = 5
KEPT = SURE[0] + SHARED + SURE[1]
CUT = (SURE[0] + SHARED - 1) * TILE
SENT = (KEPT - 1) * TILE
HALF, ALL_FIRST, LANE, AT, AT_SENT, PART = range(2 * SHARED, 2 * SHARED + 6)
BLOCK = 512
STREAM = 512
N_BLOCKS = -(-KEPT * TILE // STREAM)
BF16 = jnp.bfloat16
F32 = jnp.float32
LIMIT = 32 * 1024 * 1024
IN_VMEM = pl.BlockSpec(memory_space=pltpu.VMEM)
IN_SMEM = pl.BlockSpec(memory_space=pltpu.SMEM)
IN_PLACE = pl.BlockSpec(memory_space=pl.ANY)
NN = ((1,), (0,))
TN = ((0,), (0,))
NT = ((1,), (1,))


def dot(a, b, dims):
    return lax.dot_general(a, b, (dims, ((), ())), preferred_element_type=F32)


def call(kernel, name, **kwargs):
    return pl.pallas_call(
        kernel, name=name, compiler_params=pltpu.CompilerParams(vmem_limit_bytes=LIMIT), **kwargs)


def fill_order(order, source):
    size = order.shape[0]
    index = source(lax.broadcasted_iota(jnp.int32, (size, 1), 0))
    hit = index == lax.broadcasted_iota(jnp.int32, (size, size), 1)
    order[...] = jnp.where(hit, 1.0, 0.0).astype(BF16)


def log2(n):
    return n.bit_length() - 1


def pack_kernel(wind_ref, out_ref, order8, order4):
    rows, slots, lanes = wind_ref.shape

    @pl.when(pl.program_id(0) == 0)
    def _():
        for count, order in ((8, order8), (4, order4)):
            c = log2(count)
            fill_order(order, lambda i: (i & (count - 1)) * slots + ((i >> (c + 1)) << 1) + ((i >> c) & 1))

    eights = []
    for start in (0, 8, 16):
        count, order = (8, order8) if start < 16 else (4, order4)
        block = wind_ref[start:start + count].reshape(count * slots, lanes)
        eights.append(dot(order[...], block, NN).reshape(slots // 2, 2 * count, lanes))
    for slot in range(2):
        rows_of = [x[:, 8 * slot:8 * slot + 8] for x in eights[:2]]
        out_ref[:, 16 * slot:16 * slot + 16] = jnp.concatenate(rows_of, axis=1).astype(BF16)
    out_ref[:, 32:] = eights[2].astype(BF16)


def pack(wind):
    rows, slots, width = wind.shape
    lanes = width // 2
    return call(
        pack_kernel,
        "pack",
        grid=(2,),
        out_shape=pltpu.HBM((slots // 2, rows * 2, width), BF16),
        in_specs=[pl.BlockSpec((rows, slots, lanes), lambda i: (0, 0, i))],
        out_specs=pl.BlockSpec((slots // 2, rows * 2, lanes), lambda i: (0, 0, i)),
        scratch_shapes=[
            pltpu.VMEM((8 * slots, 8 * slots), BF16),
            pltpu.VMEM((4 * slots, 4 * slots), BF16),
        ],
    )(*in_hbm(wind))


def unpack_kernel(halves, payload, *refs):
    rot_ref, div_ref, outs, order8, order4, sems = refs[-6:]
    _, rows, slots, lanes = outs.shape
    for count, order in ((8, order8), (4, order4)):
        c = log2(count)

        def source(i):
            slot = i & (slots - 1)
            return ((slot >> 1) << (c + 1)) + ((slot & 1) << c) + (i >> log2(slots))

        fill_order(order, source)
    copies = []
    for part in range(2):
        cols = slice(2 * part * lanes, 2 * (part + 1) * lanes)
        mains = [payload[:, 16 * slot:16 * slot + 16, cols].astype(F32) for slot in range(2)]
        for start in (0, 8, 16):
            if start < 16:
                block = jnp.concatenate([x[:, start:start + 8] for x in mains], axis=1)
                count, order = 8, order8
            else:
                block = payload[:, 32:, cols].astype(F32)
                count, order = 4, order4
            moved = dot(order[...], block.reshape(count * slots, 2 * lanes).astype(BF16), NN)
            moved = moved.reshape(count, slots, 2 * lanes).astype(BF16)
            for k in range(2):
                outs[2 * part + k, start:start + count] = moved[:, :, k * lanes:(k + 1) * lanes]
        for k, component in enumerate((part, 3 - part)):
            n = 2 * part + k
            at = (slice(None), slice(None), pl.ds(component * lanes, lanes))
            copies.append([pltpu.make_async_copy(outs.at[n], ref.at[at], sems.at[n]) for ref in (rot_ref, div_ref)])
            for half in range(2):
                pl.when(halves[part] == half)(copies[n][half].start)
    for to_rot, _ in copies:
        to_rot.wait()


def unpack(halves, payload, rows, filled=()):
    pairs, both, width = payload.shape
    slots = pairs * 2
    shape = (rows, slots, width)
    return call(
        unpack_kernel,
        "unpack",
        out_shape=(pltpu.HBM(shape, BF16), pltpu.HBM(shape, BF16)),
        in_specs=[IN_SMEM, IN_VMEM] + [IN_PLACE] * len(filled),
        out_specs=(IN_PLACE, IN_PLACE),
        input_output_aliases={2: 0, 3: 1} if filled else {},
        scratch_shapes=[
            pltpu.VMEM((4, rows, slots, width // 4), BF16),
            pltpu.VMEM((8 * slots, 8 * slots), BF16),
            pltpu.VMEM((4 * slots, 4 * slots), BF16),
            pltpu.SemaphoreType.DMA((4,)),
        ],
    )(halves, payload, *filled)


def in_hbm(*arrays):
    return [pltpu.with_memory_space_constraint(x, pltpu.HBM) for x in arrays]


def keep_kernel(meta, select, p_ref, h_ref, out_ref, kept, moved, sems, out_sems):
    quarter, degrees = p_ref.shape[1:]
    pieces = [(0, degrees - SURE[0] * TILE, SURE[0], 0)]
    for k in range(SHARED):
        pieces.append((meta[k], pl.multiple_of(meta[SHARED + k] * TILE, TILE), 1, SURE[0] + k))
    pieces.append((1, degrees - SURE[1] * TILE, SURE[1], SURE[0] + SHARED))
    copies = []
    for at, ref in enumerate((p_ref, h_ref)):
        for slot, source, count, target in pieces:
            copies.append(pltpu.make_async_copy(
                ref.at[slot, :, pl.ds(source, count * TILE)],
                kept.at[pl.ds(at * quarter, quarter), pl.ds(target * TILE, count * TILE)],
                sems.at[len(copies)],
            ))
            copies[-1].start()
    sent = []
    for at in range(2):
        for copy in copies[at * len(pieces):(at + 1) * len(pieces)]:
            copy.wait()
        rows = slice(at * quarter, (at + 1) * quarter)
        for n in range(N_BLOCKS):
            start, size = n * STREAM, min(STREAM, KEPT * TILE - n * STREAM)
            cols = slice(start, start + size)
            moved[rows, cols] = dot(select[...], kept[rows, cols], NN).astype(BF16)
            block = (pl.ds(at * quarter, quarter), pl.ds(start, size))
            sent.append(pltpu.make_async_copy(moved.at[block], out_ref.at[block], out_sems.at[len(sent)]))
            sent[-1].start()
    for copy in sent:
        copy.wait()


def keep(meta, select, p_table, h_table):
    shape = (2 * p_table.shape[1], KEPT * TILE)
    return call(
        keep_kernel,
        "keep",
        out_shape=pltpu.HBM(shape, BF16),
        in_specs=[IN_SMEM, IN_VMEM] + [IN_PLACE] * 2,
        out_specs=IN_PLACE,
        scratch_shapes=[
            pltpu.VMEM(shape, BF16),
            pltpu.VMEM(shape, BF16),
            pltpu.SemaphoreType.DMA((2 * (2 + SHARED),)),
            pltpu.SemaphoreType.DMA((2 * N_BLOCKS,)),
        ],
    )(meta, select, *in_hbm(p_table, h_table))


def last_rows(slot, owners):
    i = lax.broadcasted_iota(jnp.int32, (4 * owners, 1), 0)
    hit = ((i >> 2) << 3) + (i & 3) + 4 * slot == lax.broadcasted_iota(jnp.int32, (4 * owners, 8 * owners), 1)
    return jnp.where(hit, 1.0, 0.0).astype(BF16)


def forward_kernel(meta, rate, mask, weight, recv, table, factor, keep, send, *refs):
    del factor
    owners, both, width = recv.shape
    source, (table, wind, spec, sems) = table, refs
    copies = []
    for n in range(N_BLOCKS):
        cols = pl.ds(n * STREAM, min(STREAM, KEPT * TILE - n * STREAM))
        copies.append(pltpu.make_async_copy(source.at[:, cols], table.at[:, cols], sems.at[n]))
        copies[n].start()
    waited = 0
    quarter = weight.shape[0]
    levels = width // 4
    main = owners * 16
    columns = [pl.ds(pl.multiple_of(at * levels, levels), levels) for at in (meta[PART], 3 - meta[PART])]
    mixed = [recv[:, 32:, cols].astype(F32).reshape(owners * 8, levels).astype(BF16) for cols in columns]
    mixed = jnp.concatenate(mixed, axis=1)
    for slot in range(2):
        rows = [recv[:, 16 * slot:16 * slot + 16, cols].reshape(main, levels).astype(F32) for cols in columns]
        rows = [jnp.concatenate(rows, axis=1), dot(last_rows(slot, owners), mixed, NN)]
        weighted = jnp.concatenate(rows, axis=0) * weight[...]
        wind[slot] = weighted.T.astype(BF16)
    split = (SURE[0] + SHARED) * TILE
    for slot in range(2):
        low, high = (0, split) if slot == 0 else (SURE[0] * TILE, KEPT * TILE)
        r = rate[slot]
        w = wind[slot]
        for start in range(low, high, BLOCK):
            cols = slice(start, min(start + BLOCK, high))
            while waited < len(copies) and waited * STREAM < cols.stop:
                copies[waited].wait()
                waited += 1
            proj_p = dot(w, table[:quarter, cols], NN)
            proj_h = dot(w, table[quarter:, cols], NN)
            psi = proj_h[:levels] - r * proj_p[levels:]
            chi = r * proj_p[:levels] - proj_h[levels:]
            if slot == 1 and start < split:
                first = mask[:, cols] > 0.5
                psi = jnp.where(first, spec[:levels, cols], psi)
                chi = jnp.where(first, spec[levels:, cols], chi)
            spec[:levels, cols] = psi
            spec[levels:, cols] = chi
    lane = lax.broadcasted_iota(jnp.int32, (2 * levels, TILE), 1)
    at = pl.ds(pl.multiple_of(meta[AT] * TILE, TILE), TILE)
    last, other = spec[:, CUT:CUT + TILE], spec[:, at]
    all_first = meta[ALL_FIRST] == 1
    low_first, low_second = jnp.where(all_first, last, other), jnp.where(all_first, other, last)
    spec[:, at] = jnp.where(lane >= meta[LANE], low_first, pltpu.roll(low_second, meta[LANE], 1))
    mine = pl.multiple_of(meta[HALF] * levels, levels)
    for ref, start in ((keep, mine), (send, levels - mine)):
        rows = pl.ds(pl.multiple_of(start, levels), levels)
        ref[:, :CUT] = spec[rows, :CUT].astype(ref.dtype)
        ref[:, CUT:] = spec[rows, CUT + TILE:].astype(ref.dtype)


def forward(last, meta, rate, mask, weight, recv, table, factor):
    owners, both, width = recv.shape
    levels = width // 4
    quarter = weight.shape[0]
    out_shape = [jax.ShapeDtypeStruct((levels, SENT), F32), jax.ShapeDtypeStruct((levels, SENT), BF16)]
    scratch = [
        pltpu.VMEM((2, 2 * levels, quarter), BF16),
        pltpu.VMEM((2 * levels, KEPT * TILE), F32),
        pltpu.SemaphoreType.DMA((N_BLOCKS,)),
    ]
    (scratch, out_shape)[last].insert((0, 2)[last], pltpu.VMEM(table.shape, BF16))
    return call(
        forward_kernel,
        "forward",
        in_specs=[IN_SMEM] * 2 + [IN_VMEM] * 3 + [IN_PLACE] * 2,
        out_specs=[IN_VMEM] * len(out_shape),
        out_shape=out_shape,
        scratch_shapes=scratch,
        cost_estimate=pl.CostEstimate(flops=5 * 10**9, bytes_accessed=10**7, transcendentals=0),
    )(meta, rate, mask, weight, recv, *in_hbm(table), factor)


def backward_kernel(meta, halves, rate, mask, first_part, second_part, table, out_ref, every, masked, last, out, sems):
    levels = first_part.shape[0]
    quarter = table.shape[0] // 2
    owners = out.shape[0]
    main = owners * 16
    split = (SURE[0] + SHARED) * TILE
    degrees = KEPT * TILE
    every[:levels] = first_part[...]
    every[levels:] = second_part[...]
    shared = slice(SURE[0] * TILE, split)
    cut = CUT - shared.start
    first = mask[:, shared.start:CUT] > 0.5
    both_slots = every[:, shared.start:CUT].astype(F32)
    lane = lax.broadcasted_iota(jnp.int32, (2 * levels, TILE), 1)
    joint = every[:, pl.ds(pl.multiple_of(meta[AT_SENT] * TILE, TILE), TILE)].astype(F32)
    back = TILE - meta[LANE]
    low_first = jnp.where(lane >= meta[LANE], joint, 0.0).astype(BF16)
    low_second = jnp.where(lane >= back, pltpu.roll(joint, back & (TILE - 1), 1), 0.0).astype(BF16)
    masked[0, :, :shared.start] = every[:, :shared.start]
    masked[0, :, shared.start:CUT] = jnp.where(first, both_slots, 0.0).astype(BF16)
    masked[1, :, :cut] = jnp.where(first, 0.0, both_slots).astype(BF16)
    masked[1, :, cut + TILE:degrees - shared.start] = every[:, CUT:]

    @pl.when(meta[ALL_FIRST] == 1)
    def _():
        masked[0, :, CUT:split] = low_first
        masked[1, :, cut:cut + TILE] = jnp.zeros_like(low_second)
        masked[1, :, cut + TILE:cut + 2 * TILE] = low_second

    @pl.when(meta[ALL_FIRST] != 1)
    def _():
        masked[0, :, CUT:split] = jnp.zeros_like(low_first)
        masked[0, :, pl.ds(pl.multiple_of(meta[AT] * TILE, TILE), TILE)] = low_first
        masked[1, :, cut:cut + TILE] = low_second

    for slot in range(2):
        low, high = (0, split) if slot == 0 else (shared.start, degrees)
        pot = masked[slot, :, :high - low]
        sum_p, sum_h = [dot(table[n * quarter:(n + 1) * quarter, low:high], pot, NT) for n in range(2)]
        for part in range(2):
            cols = slice(part * levels, (part + 1) * levels)
            r = rate[slot] if part == 0 else -rate[slot]
            p, h = r * sum_p[:, cols], sum_h[:, cols]
            of_psi = halves[part] == 0
            for n, field in enumerate((jnp.where(of_psi, -h, -p), jnp.where(of_psi, p, h))):
                field = field.astype(BF16)
                at = slice((2 * part + n) * levels, (2 * part + n + 1) * levels)
                out[:, 16 * slot:16 * slot + 16, at] = field[:main].reshape(owners, 16, levels)
                last[slot, :, at] = field[main:]
    mixed = dot(last_rows(0, owners), last[0], TN) + dot(last_rows(1, owners), last[1], TN)
    out[:, 32:] = mixed.reshape(owners, 8, 4 * levels).astype(BF16)
    sent = []
    for n, part in enumerate((meta[PART], 1 - meta[PART])):
        column = pl.multiple_of(part * 2 * levels, 2 * levels)
        sent.append(pltpu.make_async_copy(
            out.at[:, :, pl.ds(n * 2 * levels, 2 * levels)], out_ref.at[:, :, pl.ds(column, 2 * levels)], sems.at[n]))
        sent[n].start()
    for copy in sent:
        copy.wait()


def backward(meta, halves, rate, mask, first_part, second_part, table, payload, flops):
    levels = first_part.shape[0]
    owners, both, width = payload
    return call(
        backward_kernel,
        "backward",
        in_specs=[IN_SMEM] * 3 + [IN_VMEM] * 4,
        out_specs=IN_PLACE,
        out_shape=pltpu.HBM(payload, BF16),
        scratch_shapes=[
            pltpu.VMEM((2 * levels, SENT), BF16),
            pltpu.VMEM((2, 2 * levels, (SURE[0] + SHARED) * TILE), BF16),
            pltpu.VMEM((2, owners * 4, 4 * levels), BF16),
            pltpu.VMEM(payload, BF16),
            pltpu.SemaphoreType.DMA((2,)),
        ],
        cost_estimate=pl.CostEstimate(flops=flops, bytes_accessed=10**7, transcendentals=0),
    )(meta, halves, rate, mask, first_part, second_part, table)


def add_kernel(kept, got, total, sent):
    total[...] = kept[...] + got[...].astype(F32)
    sent[...] = total[...].astype(BF16)


def add(kept, got):
    return call(
        add_kernel,
        "add",
        in_specs=[IN_VMEM] * 2,
        out_specs=[IN_VMEM] * 2,
        out_shape=[jax.ShapeDtypeStruct(kept.shape, F32), jax.ShapeDtypeStruct(kept.shape, BF16)],
    )(kept, got)


def scale_kernel(kept, got, factor, mine):
    mine[...] = ((kept[...] + got[...].astype(F32)) * factor[...]).astype(BF16)


def scale(kept, got, factor):
    return call(
        scale_kernel,
        "scale",
        in_specs=[IN_VMEM] * 3,
        out_specs=IN_VMEM,
        out_shape=jax.ShapeDtypeStruct(kept.shape, BF16),
    )(kept, got, factor)


def relay_kernel(x, out):
    out[...] = x[...]


def relay(x):
    return call(
        relay_kernel,
        "relay",
        in_specs=[IN_VMEM],
        out_specs=IN_VMEM,
        out_shape=jax.ShapeDtypeStruct(x.shape, x.dtype),
        cost_estimate=pl.CostEstimate(flops=10**10, bytes_accessed=10**6, transcendentals=0),
    )(x)


def layout(wavenumbers, count, half, part):
    low_first, low_second = wavenumbers[0] // TILE, wavenumbers[1] // TILE
    n_first = count - low_first - SURE[0]
    k = jnp.arange(SHARED)
    shared_slot = (k >= n_first).astype(jnp.int32)
    shared_tile = jnp.where(k < n_first, count - SURE[0] - 1 - k, count - SURE[1] - 1 - (k - n_first))
    slot = jnp.concatenate([jnp.zeros(SURE[0], jnp.int32), shared_slot, jnp.ones(SURE[1], jnp.int32)])
    mask = jnp.repeat(1.0 - slot.astype(F32), TILE)[None, :]
    all_first = n_first == SHARED
    at = jnp.where(n_first == 0, 0, SURE[0] - 1 + n_first)
    at, at_sent = jnp.where(all_first, SURE[0] + SHARED, at), jnp.where(all_first, SURE[0] + SHARED - 1, at)
    lane_first = wavenumbers[0] % TILE
    scalars = jnp.stack([half, all_first.astype(jnp.int32), lane_first, at, at_sent, part])
    meta = jnp.concatenate([shared_slot, shared_tile, scalars]).astype(jnp.int32)
    tile = jnp.concatenate([jnp.arange(count - SURE[0], count), shared_tile[:-1], jnp.arange(count - SURE[1], count)])
    joint = jnp.arange(tile.shape[0]) == at_sent
    lane = jnp.arange(TILE)
    degree = jnp.where(joint, low_first, tile)[:, None] * TILE + lane[None, :]
    degree_second = low_second * TILE + TILE + lane - lane_first
    degree = jnp.where(joint[:, None] & (lane < lane_first)[None, :], degree_second[None, :], degree).astype(F32)
    factor = (-(LMAX * LMAX * 1.0) / jnp.maximum(degree * (degree + 1.0), 1.0)).reshape(1, -1)
    return meta, mask, factor


def on_device(fourier_wind, quad_weight, p_table, h_table, wavenumbers, row_latitude):
    owners = lax.axis_size("ma")
    groups = lax.axis_size("oct")
    me = lax.axis_index("oct")
    rows = fourier_wind.shape[0]
    quarter = p_table.shape[1]
    count = p_table.shape[2] // TILE
    flip, turn = [z ^ 1 for z in range(groups)], [groups - 1 - z for z in range(groups)]
    ways = [
        [(d * groups + z, d * groups + (flip, turn)[(d + n) % 2][z]) for d in range(owners) for z in range(groups)]
        for n in range(2)]
    halves = ((me + 1) // 2) % 2, me // 2
    odd = lax.axis_index("ma") % 2

    def swap(x, pairs):
        return lax.ppermute(x, ("ma", "oct"), pairs)

    received = lax.all_to_all(pack(fourier_wind), "ma", 0, 0, tiled=True)

    metas = []
    for n in range(2):
        half = jnp.where(odd == n, *halves)
        meta, mask, factor = layout(wavenumbers, count, half, odd ^ n)
        metas.append(meta)
    rate = wavenumbers.astype(F32) / LMAX

    local = lax.dynamic_index_in_dim(row_latitude.reshape(owners, groups, rows), me, 1, keepdims=False) - me * quarter
    target = jnp.concatenate([local[:, :16].reshape(-1), local[:, 16:].reshape(-1)])[:, None]
    hit = target == jnp.arange(quarter)[None, :]
    weight = jnp.sum(jnp.where(hit, quad_weight[None, :], 0.0), axis=1, keepdims=True)
    table = keep(meta, hit.astype(BF16), p_table, h_table)
    owners, both, width = received.shape
    rate = jnp.where(odd == 0, rate, -rate)
    signs = (rate, -rate)
    kept_a, sent_a = forward(0, metas[0], signs[0], mask, weight, received, table, factor)
    kept_b, sent_b, table = forward(1, metas[1], signs[1], mask, weight, received, table, factor)
    table = pltpu.with_memory_space_constraint(table, pltpu.VMEM)
    kept_a, sent_a = add(kept_a, swap(sent_a, ways[0]))
    kept_b, sent_b = add(kept_b, swap(sent_b, ways[1]))
    mine_a = scale(kept_a, swap(sent_a, ways[1]), factor)
    mine_b = scale(kept_b, swap(sent_b, ways[0]), factor)
    kept_halves = jnp.stack([meta[HALF] for meta in metas])
    theirs_a = swap(mine_a, ways[0])
    kept = backward(metas[0], kept_halves, rate, mask, mine_a, mine_b, table, received.shape, 50000000000)
    mine_b, kept = lax.optimization_barrier((mine_b, kept))
    theirs_b = swap(mine_b, ways[1])
    theirs_a = relay(theirs_a)
    others = backward(metas[0], 1 - kept_halves, rate, mask, theirs_a, theirs_b, table, received.shape, 2000000000)
    kept, others = (lax.all_to_all(x, "ma", 0, 0, tiled=True) for x in (kept, others))
    halves = jnp.stack(halves).astype(jnp.int32)
    return tuple(unpack(1 - halves, others, rows, unpack(halves, kept, rows)))


def solution(mesh):
    placed = (
        P(("ma", "oct"), None, None),
        P("oct"),
        P("ma", "oct", None),
        P("ma", "oct", None),
        P("ma"),
        P(),
    )
    return jax.shard_map(
        on_device,
        mesh=mesh,
        in_specs=placed,
        out_specs=(P(("ma", "oct"), None, None), P(("ma", "oct"), None, None)),
        check_vma=False,
    )
```

```python
import functools

import jax
import jax.numpy as jnp
from jax import lax
from jax.experimental import pallas as pl
from jax.experimental.pallas import tpu as pltpu
from jax.sharding import PartitionSpec as P

LMAX = 2559
TILE = 128
SURE = (11, 5)
SHARED = 5
KEPT = SURE[0] + SHARED + SURE[1]
CUT = (SURE[0] + SHARED - 1) * TILE
SENT = (KEPT - 1) * TILE
HALF, ALL_FIRST, LANE, AT, AT_SENT, PART = range(2 * SHARED, 2 * SHARED + 6)
BLOCK = 512
STREAM = 512
N_BLOCKS = -(-KEPT * TILE // STREAM)
BF16 = jnp.bfloat16
F32 = jnp.float32
LIMIT = 32 * 1024 * 1024
IN_VMEM = pl.BlockSpec(memory_space=pltpu.VMEM)
IN_SMEM = pl.BlockSpec(memory_space=pltpu.SMEM)
IN_PLACE = pl.BlockSpec(memory_space=pl.ANY)
NN = ((1,), (0,))
TN = ((0,), (0,))
NT = ((1,), (1,))


def dot(a, b, dims):
    return lax.dot_general(a, b, (dims, ((), ())), preferred_element_type=F32)


def call(kernel, name, **kwargs):
    return pl.pallas_call(
        kernel, name=name, compiler_params=pltpu.CompilerParams(vmem_limit_bytes=LIMIT), **kwargs)


def fill_order(order, source):
    size = order.shape[0]
    index = source(lax.broadcasted_iota(jnp.int32, (size, 1), 0))
    hit = index == lax.broadcasted_iota(jnp.int32, (size, size), 1)
    order[...] = jnp.where(hit, 1.0, 0.0).astype(BF16)


def log2(n):
    return n.bit_length() - 1


def pack_kernel(wind_ref, out_ref, order8, order4):
    rows, slots, lanes = wind_ref.shape

    @pl.when(pl.program_id(0) == 0)
    def _():
        for count, order in ((8, order8), (4, order4)):
            c = log2(count)
            fill_order(order, lambda i: (i & (count - 1)) * slots + ((i >> (c + 1)) << 1) + ((i >> c) & 1))

    eights = []
    for start in (0, 8, 16):
        count, order = (8, order8) if start < 16 else (4, order4)
        block = wind_ref[start:start + count].reshape(count * slots, lanes)
        eights.append(dot(order[...], block, NN).reshape(slots // 2, 2 * count, lanes))
    for slot in range(2):
        rows_of = [x[:, 8 * slot:8 * slot + 8] for x in eights[:2]]
        out_ref[:, 16 * slot:16 * slot + 16] = jnp.concatenate(rows_of, axis=1).astype(BF16)
    out_ref[:, 32:] = eights[2].astype(BF16)


def pack(wind):
    rows, slots, width = wind.shape
    lanes = width // 2
    return call(
        pack_kernel,
        "pack",
        grid=(2,),
        out_shape=pltpu.HBM((slots // 2, rows * 2, width), BF16),
        in_specs=[pl.BlockSpec((rows, slots, lanes), lambda i: (0, 0, i))],
        out_specs=pl.BlockSpec((slots // 2, rows * 2, lanes), lambda i: (0, 0, i)),
        scratch_shapes=[
            pltpu.VMEM((8 * slots, 8 * slots), BF16),
            pltpu.VMEM((4 * slots, 4 * slots), BF16),
        ],
    )(*in_hbm(wind))


def unpack_kernel(halves, payload, *refs):
    rot_ref, div_ref, outs, order8, order4, sems = refs[-6:]
    _, rows, slots, lanes = outs.shape
    for count, order in ((8, order8), (4, order4)):
        c = log2(count)

        def source(i):
            slot = i & (slots - 1)
            return ((slot >> 1) << (c + 1)) + ((slot & 1) << c) + (i >> log2(slots))

        fill_order(order, source)
    copies = []
    for part in range(2):
        cols = slice(2 * part * lanes, 2 * (part + 1) * lanes)
        mains = [payload[:, 16 * slot:16 * slot + 16, cols].astype(F32) for slot in range(2)]
        for start in (0, 8, 16):
            if start < 16:
                block = jnp.concatenate([x[:, start:start + 8] for x in mains], axis=1)
                count, order = 8, order8
            else:
                block = payload[:, 32:, cols].astype(F32)
                count, order = 4, order4
            moved = dot(order[...], block.reshape(count * slots, 2 * lanes).astype(BF16), NN)
            moved = moved.reshape(count, slots, 2 * lanes).astype(BF16)
            for k in range(2):
                outs[2 * part + k, start:start + count] = moved[:, :, k * lanes:(k + 1) * lanes]
        for k, component in enumerate((part, 3 - part)):
            n = 2 * part + k
            at = (slice(None), slice(None), pl.ds(component * lanes, lanes))
            copies.append([pltpu.make_async_copy(outs.at[n], ref.at[at], sems.at[n]) for ref in (rot_ref, div_ref)])
            for half in range(2):
                pl.when(halves[part] == half)(copies[n][half].start)
    for to_rot, _ in copies:
        to_rot.wait()


def unpack(halves, payload, rows, filled=()):
    pairs, both, width = payload.shape
    slots = pairs * 2
    shape = (rows, slots, width)
    return call(
        unpack_kernel,
        "unpack",
        out_shape=(pltpu.HBM(shape, BF16), pltpu.HBM(shape, BF16)),
        in_specs=[IN_SMEM, IN_VMEM] + [IN_PLACE] * len(filled),
        out_specs=(IN_PLACE, IN_PLACE),
        input_output_aliases={2: 0, 3: 1} if filled else {},
        scratch_shapes=[
            pltpu.VMEM((4, rows, slots, width // 4), BF16),
            pltpu.VMEM((8 * slots, 8 * slots), BF16),
            pltpu.VMEM((4 * slots, 4 * slots), BF16),
            pltpu.SemaphoreType.DMA((4,)),
        ],
    )(halves, payload, *filled)


def in_hbm(*arrays):
    return [pltpu.with_memory_space_constraint(x, pltpu.HBM) for x in arrays]


def keep_kernel(meta, select, p_ref, h_ref, out_ref, kept, moved, sems, out_sems):
    quarter, degrees = p_ref.shape[1:]
    pieces = [(0, degrees - SURE[0] * TILE, SURE[0], 0)]
    for k in range(SHARED):
        pieces.append((meta[k], pl.multiple_of(meta[SHARED + k] * TILE, TILE), 1, SURE[0] + k))
    pieces.append((1, degrees - SURE[1] * TILE, SURE[1], SURE[0] + SHARED))
    copies = []
    for at, ref in enumerate((p_ref, h_ref)):
        for slot, source, count, target in pieces:
            copies.append(pltpu.make_async_copy(
                ref.at[slot, :, pl.ds(source, count * TILE)],
                kept.at[pl.ds(at * quarter, quarter), pl.ds(target * TILE, count * TILE)],
                sems.at[len(copies)],
            ))
            copies[-1].start()
    sent = []
    for at in range(2):
        for copy in copies[at * len(pieces):(at + 1) * len(pieces)]:
            copy.wait()
        rows = slice(at * quarter, (at + 1) * quarter)
        for n in range(N_BLOCKS):
            start, size = n * STREAM, min(STREAM, KEPT * TILE - n * STREAM)
            cols = slice(start, start + size)
            moved[rows, cols] = dot(select[...], kept[rows, cols], NN).astype(BF16)
            block = (pl.ds(at * quarter, quarter), pl.ds(start, size))
            sent.append(pltpu.make_async_copy(moved.at[block], out_ref.at[block], out_sems.at[len(sent)]))
            sent[-1].start()
    for copy in sent:
        copy.wait()


def keep(meta, select, p_table, h_table):
    shape = (2 * p_table.shape[1], KEPT * TILE)
    return call(
        keep_kernel,
        "keep",
        out_shape=pltpu.HBM(shape, BF16),
        in_specs=[IN_SMEM, IN_VMEM] + [IN_PLACE] * 2,
        out_specs=IN_PLACE,
        scratch_shapes=[
            pltpu.VMEM(shape, BF16),
            pltpu.VMEM(shape, BF16),
            pltpu.SemaphoreType.DMA((2 * (2 + SHARED),)),
            pltpu.SemaphoreType.DMA((2 * N_BLOCKS,)),
        ],
    )(meta, select, *in_hbm(p_table, h_table))


def last_rows(slot, owners):
    i = lax.broadcasted_iota(jnp.int32, (4 * owners, 1), 0)
    hit = ((i >> 2) << 3) + (i & 3) + 4 * slot == lax.broadcasted_iota(jnp.int32, (4 * owners, 8 * owners), 1)
    return jnp.where(hit, 1.0, 0.0).astype(BF16)


def forward_kernel(meta, rate, mask, weight, recv, table, factor, keep, send, *refs):
    del factor
    owners, both, width = recv.shape
    source, (table, wind, spec, sems) = table, refs
    copies = []
    for n in range(N_BLOCKS):
        cols = pl.ds(n * STREAM, min(STREAM, KEPT * TILE - n * STREAM))
        copies.append(pltpu.make_async_copy(source.at[:, cols], table.at[:, cols], sems.at[n]))
        copies[n].start()
    waited = 0
    quarter = weight.shape[0]
    levels = width // 4
    main = owners * 16
    columns = [pl.ds(pl.multiple_of(at * levels, levels), levels) for at in (meta[PART], 3 - meta[PART])]
    mixed = [recv[:, 32:, cols].astype(F32).reshape(owners * 8, levels).astype(BF16) for cols in columns]
    mixed = jnp.concatenate(mixed, axis=1)
    for slot in range(2):
        rows = [recv[:, 16 * slot:16 * slot + 16, cols].reshape(main, levels).astype(F32) for cols in columns]
        rows = [jnp.concatenate(rows, axis=1), dot(last_rows(slot, owners), mixed, NN)]
        weighted = jnp.concatenate(rows, axis=0) * weight[...]
        wind[slot] = weighted.T.astype(BF16)
    split = (SURE[0] + SHARED) * TILE
    for slot in range(2):
        low, high = (0, split) if slot == 0 else (SURE[0] * TILE, KEPT * TILE)
        r = rate[slot]
        w = wind[slot]
        for start in range(low, high, BLOCK):
            cols = slice(start, min(start + BLOCK, high))
            while waited < len(copies) and waited * STREAM < cols.stop:
                copies[waited].wait()
                waited += 1
            proj_p = dot(w, table[:quarter, cols], NN)
            proj_h = dot(w, table[quarter:, cols], NN)
            psi = proj_h[:levels] - r * proj_p[levels:]
            chi = r * proj_p[:levels] - proj_h[levels:]
            if slot == 1 and start < split:
                first = mask[:, cols] > 0.5
                psi = jnp.where(first, spec[:levels, cols], psi)
                chi = jnp.where(first, spec[levels:, cols], chi)
            spec[:levels, cols] = psi
            spec[levels:, cols] = chi
    lane = lax.broadcasted_iota(jnp.int32, (2 * levels, TILE), 1)
    at = pl.ds(pl.multiple_of(meta[AT] * TILE, TILE), TILE)
    last, other = spec[:, CUT:CUT + TILE], spec[:, at]
    all_first = meta[ALL_FIRST] == 1
    low_first, low_second = jnp.where(all_first, last, other), jnp.where(all_first, other, last)
    spec[:, at] = jnp.where(lane >= meta[LANE], low_first, pltpu.roll(low_second, meta[LANE], 1))
    mine = pl.multiple_of(meta[HALF] * levels, levels)
    for ref, start in ((keep, mine), (send, levels - mine)):
        rows = pl.ds(pl.multiple_of(start, levels), levels)
        ref[:, :CUT] = spec[rows, :CUT].astype(ref.dtype)
        ref[:, CUT:] = spec[rows, CUT + TILE:].astype(ref.dtype)


def forward(last, meta, rate, mask, weight, recv, table, factor):
    owners, both, width = recv.shape
    levels = width // 4
    quarter = weight.shape[0]
    out_shape = [jax.ShapeDtypeStruct((levels, SENT), F32), jax.ShapeDtypeStruct((levels, SENT), BF16)]
    scratch = [
        pltpu.VMEM((2, 2 * levels, quarter), BF16),
        pltpu.VMEM((2 * levels, KEPT * TILE), F32),
        pltpu.SemaphoreType.DMA((N_BLOCKS,)),
    ]
    (scratch, out_shape)[last].insert((0, 2)[last], pltpu.VMEM(table.shape, BF16))
    return call(
        forward_kernel,
        "forward",
        in_specs=[IN_SMEM] * 2 + [IN_VMEM] * 3 + [IN_PLACE] * 2,
        out_specs=[IN_VMEM] * len(out_shape),
        out_shape=out_shape,
        scratch_shapes=scratch,
        cost_estimate=pl.CostEstimate(flops=5 * 10**9, bytes_accessed=10**7, transcendentals=0),
    )(meta, rate, mask, weight, recv, *in_hbm(table), factor)


def backward_kernel(passes, meta, halves, rate, mask, first_part, second_part, table, out_ref, *refs):
    every, masked, last, out, sems = refs[passes:passes + 5]
    if passes:
        passed = pltpu.make_async_copy(second_part, refs[0], refs[-1])
        passed.start()
    levels = first_part.shape[0]
    quarter = table.shape[0] // 2
    owners = out.shape[0]
    main = owners * 16
    split = (SURE[0] + SHARED) * TILE
    degrees = KEPT * TILE
    every[:levels] = first_part[...]
    every[levels:] = second_part[...]
    shared = slice(SURE[0] * TILE, split)
    cut = CUT - shared.start
    first = mask[:, shared.start:CUT] > 0.5
    both_slots = every[:, shared.start:CUT].astype(F32)
    lane = lax.broadcasted_iota(jnp.int32, (2 * levels, TILE), 1)
    joint = every[:, pl.ds(pl.multiple_of(meta[AT_SENT] * TILE, TILE), TILE)].astype(F32)
    back = TILE - meta[LANE]
    low_first = jnp.where(lane >= meta[LANE], joint, 0.0).astype(BF16)
    low_second = jnp.where(lane >= back, pltpu.roll(joint, back & (TILE - 1), 1), 0.0).astype(BF16)
    masked[0, :, :shared.start] = every[:, :shared.start]
    masked[0, :, shared.start:CUT] = jnp.where(first, both_slots, 0.0).astype(BF16)
    masked[1, :, :cut] = jnp.where(first, 0.0, both_slots).astype(BF16)
    masked[1, :, cut + TILE:degrees - shared.start] = every[:, CUT:]

    @pl.when(meta[ALL_FIRST] == 1)
    def _():
        masked[0, :, CUT:split] = low_first
        masked[1, :, cut:cut + TILE] = jnp.zeros_like(low_second)
        masked[1, :, cut + TILE:cut + 2 * TILE] = low_second

    @pl.when(meta[ALL_FIRST] != 1)
    def _():
        masked[0, :, CUT:split] = jnp.zeros_like(low_first)
        masked[0, :, pl.ds(pl.multiple_of(meta[AT] * TILE, TILE), TILE)] = low_first
        masked[1, :, cut:cut + TILE] = low_second

    for slot in range(2):
        low, high = (0, split) if slot == 0 else (shared.start, degrees)
        pot = masked[slot, :, :high - low]
        sum_p, sum_h = [dot(table[n * quarter:(n + 1) * quarter, low:high], pot, NT) for n in range(2)]
        for part in range(2):
            cols = slice(part * levels, (part + 1) * levels)
            r = rate[slot] if part == 0 else -rate[slot]
            p, h = r * sum_p[:, cols], sum_h[:, cols]
            of_psi = halves[part] == 0
            for n, field in enumerate((jnp.where(of_psi, -h, -p), jnp.where(of_psi, p, h))):
                field = field.astype(BF16)
                at = slice((2 * part + n) * levels, (2 * part + n + 1) * levels)
                out[:, 16 * slot:16 * slot + 16, at] = field[:main].reshape(owners, 16, levels)
                last[slot, :, at] = field[main:]
    mixed = dot(last_rows(0, owners), last[0], TN) + dot(last_rows(1, owners), last[1], TN)
    out[:, 32:] = mixed.reshape(owners, 8, 4 * levels).astype(BF16)
    sent = []
    for n, part in enumerate((meta[PART], 1 - meta[PART])):
        column = pl.multiple_of(part * 2 * levels, 2 * levels)
        sent.append(pltpu.make_async_copy(
            out.at[:, :, pl.ds(n * 2 * levels, 2 * levels)], out_ref.at[:, :, pl.ds(column, 2 * levels)], sems.at[n]))
        sent[n].start()
    for copy in sent:
        copy.wait()
    if passes:
        passed.wait()


def backward(passes, meta, halves, rate, mask, first_part, second_part, table, payload, flops):
    levels = first_part.shape[0]
    owners, both, width = payload
    return call(
        functools.partial(backward_kernel, passes),
        "backward",
        in_specs=[IN_SMEM] * 3 + [IN_VMEM] * 4,
        out_specs=[IN_PLACE] * (1 + passes),
        out_shape=[pltpu.HBM(payload, BF16), pltpu.HBM(second_part.shape, BF16)][:1 + passes],
        scratch_shapes=[
            pltpu.VMEM((2 * levels, SENT), BF16),
            pltpu.VMEM((2, 2 * levels, (SURE[0] + SHARED) * TILE), BF16),
            pltpu.VMEM((2, owners * 4, 4 * levels), BF16),
            pltpu.VMEM(payload, BF16),
            pltpu.SemaphoreType.DMA((2,)),
        ] + [pltpu.SemaphoreType.DMA] * passes,
        cost_estimate=pl.CostEstimate(flops=flops, bytes_accessed=10**7, transcendentals=0),
    )(meta, halves, rate, mask, first_part, second_part, table)


def add_kernel(kept, got, total, sent):
    total[...] = kept[...] + got[...].astype(F32)
    sent[...] = total[...].astype(BF16)


def add(kept, got):
    return call(
        add_kernel,
        "add",
        in_specs=[IN_VMEM] * 2,
        out_specs=[IN_VMEM] * 2,
        out_shape=[jax.ShapeDtypeStruct(kept.shape, F32), jax.ShapeDtypeStruct(kept.shape, BF16)],
    )(kept, got)


def scale_kernel(kept, got, factor, mine):
    mine[...] = ((kept[...] + got[...].astype(F32)) * factor[...]).astype(BF16)


def scale(kept, got, factor):
    return call(
        scale_kernel,
        "scale",
        in_specs=[IN_VMEM] * 3,
        out_specs=IN_VMEM,
        out_shape=jax.ShapeDtypeStruct(kept.shape, BF16),
    )(kept, got, factor)


def relay_kernel(x, out):
    out[...] = x[...]


def relay(x):
    return call(
        relay_kernel,
        "relay",
        in_specs=[IN_VMEM],
        out_specs=IN_VMEM,
        out_shape=jax.ShapeDtypeStruct(x.shape, x.dtype),
        cost_estimate=pl.CostEstimate(flops=10**10, bytes_accessed=10**6, transcendentals=0),
    )(x)


def layout(wavenumbers, count, half, part):
    low_first, low_second = wavenumbers[0] // TILE, wavenumbers[1] // TILE
    n_first = count - low_first - SURE[0]
    k = jnp.arange(SHARED)
    shared_slot = (k >= n_first).astype(jnp.int32)
    shared_tile = jnp.where(k < n_first, count - SURE[0] - 1 - k, count - SURE[1] - 1 - (k - n_first))
    slot = jnp.concatenate([jnp.zeros(SURE[0], jnp.int32), shared_slot, jnp.ones(SURE[1], jnp.int32)])
    mask = jnp.repeat(1.0 - slot.astype(F32), TILE)[None, :]
    all_first = n_first == SHARED
    at = jnp.where(n_first == 0, 0, SURE[0] - 1 + n_first)
    at, at_sent = jnp.where(all_first, SURE[0] + SHARED, at), jnp.where(all_first, SURE[0] + SHARED - 1, at)
    lane_first = wavenumbers[0] % TILE
    scalars = jnp.stack([half, all_first.astype(jnp.int32), lane_first, at, at_sent, part])
    meta = jnp.concatenate([shared_slot, shared_tile, scalars]).astype(jnp.int32)
    tile = jnp.concatenate([jnp.arange(count - SURE[0], count), shared_tile[:-1], jnp.arange(count - SURE[1], count)])
    joint = jnp.arange(tile.shape[0]) == at_sent
    lane = jnp.arange(TILE)
    degree = jnp.where(joint, low_first, tile)[:, None] * TILE + lane[None, :]
    degree_second = low_second * TILE + TILE + lane - lane_first
    degree = jnp.where(joint[:, None] & (lane < lane_first)[None, :], degree_second[None, :], degree).astype(F32)
    factor = (-(LMAX * LMAX * 1.0) / jnp.maximum(degree * (degree + 1.0), 1.0)).reshape(1, -1)
    return meta, mask, factor


def on_device(fourier_wind, quad_weight, p_table, h_table, wavenumbers, row_latitude):
    owners = lax.axis_size("ma")
    groups = lax.axis_size("oct")
    me = lax.axis_index("oct")
    rows = fourier_wind.shape[0]
    quarter = p_table.shape[1]
    count = p_table.shape[2] // TILE
    flip, turn = [z ^ 1 for z in range(groups)], [groups - 1 - z for z in range(groups)]
    ways = [
        [(d * groups + z, d * groups + (flip, turn)[(d + n) % 2][z]) for d in range(owners) for z in range(groups)]
        for n in range(2)]
    halves = ((me + 1) // 2) % 2, me // 2
    odd = lax.axis_index("ma") % 2

    def swap(x, pairs):
        return lax.ppermute(x, ("ma", "oct"), pairs)

    received = lax.all_to_all(pack(fourier_wind), "ma", 0, 0, tiled=True)

    metas = []
    for n in range(2):
        half = jnp.where(odd == n, *halves)
        meta, mask, factor = layout(wavenumbers, count, half, odd ^ n)
        metas.append(meta)
    rate = wavenumbers.astype(F32) / LMAX

    local = lax.dynamic_index_in_dim(row_latitude.reshape(owners, groups, rows), me, 1, keepdims=False) - me * quarter
    target = jnp.concatenate([local[:, :16].reshape(-1), local[:, 16:].reshape(-1)])[:, None]
    hit = target == jnp.arange(quarter)[None, :]
    weight = jnp.sum(jnp.where(hit, quad_weight[None, :], 0.0), axis=1, keepdims=True)
    table = keep(meta, hit.astype(BF16), p_table, h_table)
    owners, both, width = received.shape
    rate = jnp.where(odd == 0, rate, -rate)
    signs = (rate, -rate)
    kept_a, sent_a = forward(0, metas[0], signs[0], mask, weight, received, table, factor)
    kept_b, sent_b, table = forward(1, metas[1], signs[1], mask, weight, received, table, factor)
    table = pltpu.with_memory_space_constraint(table, pltpu.VMEM)
    kept_a, sent_a = add(kept_a, swap(sent_a, ways[0]))
    kept_b, sent_b = add(kept_b, swap(sent_b, ways[1]))
    mine_a = scale(kept_a, swap(sent_a, ways[1]), factor)
    mine_b = scale(kept_b, swap(sent_b, ways[0]), factor)
    kept_halves = jnp.stack([meta[HALF] for meta in metas])
    theirs_a = swap(mine_a, ways[0])
    kept, mine_b = backward(1, metas[0], kept_halves, rate, mask, mine_a, mine_b, table, received.shape, 50000000000)
    theirs_b = swap(mine_b, ways[1])
    theirs_a = relay(theirs_a)
    others, = backward(0, metas[0], 1 - kept_halves, rate, mask, theirs_a, theirs_b, table, received.shape, 2000000000)
    kept, others = (lax.all_to_all(x, "ma", 0, 0, tiled=True) for x in (kept, others))
    halves = jnp.stack(halves).astype(jnp.int32)
    return tuple(unpack(1 - halves, others, rows, unpack(halves, kept, rows)))


def solution(mesh):
    placed = (
        P(("ma", "oct"), None, None),
        P("oct"),
        P("ma", "oct", None),
        P("ma", "oct", None),
        P("ma"),
        P(),
    )
    return jax.shard_map(
        on_device,
        mesh=mesh,
        in_specs=placed,
        out_specs=(P(("ma", "oct"), None, None), P(("ma", "oct"), None, None)),
        check_vma=False,
    )
```
